32 devices in a mesh: group: 4 (over z), tp: 4 (over y, core), fork: 2 (over x).
Axes of the slice: x: 2, y: 2, z: 4, core: 2. Of those that a mesh axis runs over, the one named last changes fastest.
Arguments:
- prompt_hidden: bfloat16 [4, 512, 8192], P(None, 'group'), may hold values from -6 to 6
- kv_weight: bfloat16 [8192, 2048], P(None, ('tp', 'fork')), may hold values from -0.0625 to 0.0625
- kv_bias: float32 [2048], P(('tp', 'fork')), may hold values from -3 to 3
- new_query: bfloat16 [4, 8, 4, 8192], P('group', ('tp', 'fork')), may hold values from -105 to 105
- new_kv: bfloat16 [4, 8, 4, 2048], P('group', ('tp', 'fork')), may hold values from -3 to 3
- decode_prompt: int32 [4], replicated, may hold values from 0 to 3, as said below
- sample_counts: int32 [4], replicated, may hold values from 1 to 8, 24 in all
- page_table: int32 [4, 64], P('group'), may hold values from 0 to 63, each once within a row
Outputs:
- attention_out: bfloat16 [4, 8, 4, 8192], P('group', ('tp', 'fork'))
- kv_cache: bfloat16 [4, 64, 8, 2048], P('group', None, None, ('tp', 'fork'))
The draws below stay inside these ranges and needn't reach their ends.
Inputs may be any that keep to these rules, and one draw needn't show every extreme that they name: `decode_prompt`: each prompt is decoded by exactly 1 group. `page_table`: each row is a permutation of the 64 slots.
All inputs are finite; a program needn't handle non-finite values.
Results may differ from the reference program's by a relative error of at most 0.0067.
Values may be sent and summed in bfloat16 or wider, within the bound.
No kernel may reach another device: no remote copies, remote signals or barrier semaphores. Data moves between devices by JAX's collectives and lax.ppermute only.
A program may use at most 128 MiB of HBM per device.

```python
import math
import jax
import jax.numpy as jnp
import numpy as np
from jax import lax

D = 8192
Q_HEADS = 64
KV_HEADS = 8
HEAD_DIM = 128
Q_PER_KV = 8
PAGE = 8
NEW = 4
DECODERS = 1
PROMPTS = 4
PLEN = 512
PAGES = 64
DSAMP = 8
SAMPLES = 8
N_GROUP = 4


def base_keys(key):
    return jnp.clip(jax.random.normal(key, (DECODERS * PROMPTS, DSAMP, NEW, KV_HEADS, HEAD_DIM), jnp.float32), -3.0, 3.0)


def draw_decode_prompt(key, part):
    key = jax.random.fold_in(key, 11)
    return (jax.random.permutation(key, DECODERS * PROMPTS) // DECODERS).astype(jnp.int32)


def draw_new_query(key, part):
    key_rows = base_keys(key)
    key = jax.random.fold_in(key, 21)
    dimensions = (DECODERS * PROMPTS, DSAMP, NEW, KV_HEADS, Q_PER_KV, HEAD_DIM)
    jitter = jnp.clip(jax.random.normal(key, dimensions, jnp.float32), -3.0, 3.0)
    queries = 1.5 * jitter + 0.5 * key_rows[:, :, :, :, None, :]
    return queries.reshape(DECODERS * PROMPTS, DSAMP, NEW, Q_HEADS * HEAD_DIM).astype(jnp.bfloat16)


def draw_new_kv(key, part):
    key_rows = base_keys(key)
    key = jax.random.fold_in(key, 33)
    dimensions = (DECODERS * PROMPTS, DSAMP, NEW, KV_HEADS, HEAD_DIM)
    values = jnp.clip(jax.random.normal(key, dimensions, jnp.float32), -3.0, 3.0)
    return jnp.stack([key_rows, values], axis=4).reshape(DECODERS * PROMPTS, DSAMP, NEW, KV_HEADS * 2 * HEAD_DIM).astype(jnp.bfloat16)


def block_levels(rng, extent, cuts, smallest, top_value):
    factor_of = 1.0
    for axis_at, parts in cuts:
        heights = jax.random.uniform(jax.random.fold_in(jax.random.fold_in(rng, 6), axis_at), (parts,), jnp.float32, smallest / len(cuts), top_value / len(cuts))
        factor_of = factor_of * jnp.repeat(jnp.exp(heights), extent[axis_at] // parts).reshape((-1,) + (1,) * (len(extent) - 1 - axis_at))
    return factor_of


def length_profile(count, total, reach, skew):
    loads = [(1 << 20) // math.isqrt(grade ** skew) + 1 for grade in range(2, count + 1)]
    surplus, counts = total - reach - (count - 1), [1] * (count - 1)
    while surplus > 0:
        movable = [i for i in range(count - 1) if counts[i] < reach]
        pool, budget = sum([loads[i] for i in movable]), surplus
        for i in movable:
            extra = min(reach - counts[i], max(1, budget * loads[i] // pool), surplus)
            counts[i] = counts[i] + extra
            surplus = surplus - extra
    return np.array([reach] + counts)


def uneven(rng, amount, total, bound, lean):
    if amount == 2:
        one = jax.random.randint(rng, (), max(1, total - bound), min(bound, total - 1) + 1)
        return jnp.stack([one, total - one])
    tallies = jnp.asarray(length_profile(amount, total, bound, lean), jnp.int32)
    pairs = (amount - 1) // 2
    donor, sink = tallies[1:1 + 2 * pairs:2], tallies[2:2 + 2 * pairs:2]
    margin = jnp.minimum(donor - 1, bound - sink)
    passed = jax.random.randint(jax.random.fold_in(rng, 1), (pairs,), 0, 1 << 20) % (margin + 1)
    tallies = tallies.at[1:1 + 2 * pairs:2].set(donor - passed).at[2:2 + 2 * pairs:2].set(sink + passed)
    return tallies[jax.random.permutation(jax.random.fold_in(rng, 2), amount)]


def bell_draw(rng, dims, deviation, limit, split=(), kind=jnp.bfloat16):
    factor_of = block_levels(rng, dims, split, -0.22, 0.18) if split else 1.0
    result = jax.random.normal(rng, dims, jnp.float32) * deviation * factor_of
    return jnp.minimum(jnp.maximum(result, -limit), limit).astype(kind)


def setup_inputs(seed: int = 0) -> dict:
    streams_of = jax.random.split(jax.random.key(seed), 9)
    return {
        "prompt_hidden": bell_draw(streams_of[0], (PROMPTS, PLEN, D), 1.0, 6.0, ((1, 4),)),
        "kv_weight": bell_draw(streams_of[1], (D, KV_HEADS * 2 * HEAD_DIM), D ** -0.5, 0.0625, ((1, 8),)),
        "kv_bias": bell_draw(streams_of[2], (KV_HEADS * 2 * HEAD_DIM,), 0.5, 3.0, ((0, 8),), jnp.float32),
        "new_query": draw_new_query(jax.random.fold_in(streams_of[8], 71), 0),
        "new_kv": draw_new_kv(jax.random.fold_in(streams_of[8], 71), 0),
        "decode_prompt": draw_decode_prompt(jax.random.fold_in(streams_of[8], 71), 0),
        "sample_counts": uneven(streams_of[6], PROMPTS, 3 * SAMPLES * PROMPTS // 4, SAMPLES, 0).astype(jnp.int32),
        "page_table": jax.vmap(lambda own: jax.random.permutation(own, PAGES))(jax.random.split(streams_of[7], N_GROUP)).reshape((N_GROUP, PAGES)).astype(jnp.int32),
    }


rope_base = 1000000.0


def rotate(vectors, positions):
    half_dim = HEAD_DIM // 2
    frequency = rope_base ** (-(2.0 * jnp.arange(half_dim, dtype=jnp.float32)) / HEAD_DIM)
    angles = positions.astype(jnp.float32)[:, None, None] * frequency[None, None, :]
    cosine = jnp.cos(angles)
    sine_of = jnp.sin(angles)
    leading = vectors[..., :half_dim]
    trailing = vectors[..., half_dim:]
    return jnp.concatenate([leading * cosine - trailing * sine_of, trailing * cosine + leading * sine_of], axis=-1)


def prompt_keys(prompt_rows, kv_weight, kv_bias):
    projected = jnp.dot(prompt_rows, kv_weight, preferred_element_type=jnp.float32) + kv_bias
    projected = projected.reshape(PLEN, KV_HEADS, 2, HEAD_DIM)
    rotated = rotate(projected[:, :, 0], jnp.arange(PLEN, dtype=jnp.int32))
    stacked = jnp.stack([rotated, projected[:, :, 1]], axis=2)
    return stacked.astype(jnp.bfloat16).reshape(PLEN, KV_HEADS * 2 * HEAD_DIM)


def attend(queries, recent_keys, recent_values, history):
    scaling = HEAD_DIM ** -0.5
    past_keys = history[:, :, :HEAD_DIM].astype(jnp.float32)
    past_values = history[:, :, HEAD_DIM:].astype(jnp.float32)
    queries = queries.astype(jnp.float32)
    past_scores = jnp.einsum("snhge,lhe->snhgl", queries, past_keys) * scaling
    recent_scores = jnp.einsum("snhge,smhe->snhgm", queries, recent_keys.astype(jnp.float32)) * scaling
    offsets = jnp.arange(NEW, dtype=jnp.int32)
    visible = offsets[:, None] >= offsets[None, :]
    recent_scores = jnp.where(visible[None, :, None, None, :], recent_scores, -jnp.inf)
    highest = jnp.maximum(jnp.max(past_scores, axis=-1), jnp.max(recent_scores, axis=-1))[..., None]
    past_weight = jnp.exp(past_scores - highest)
    recent_weight = jnp.exp(recent_scores - highest)
    denominator = jnp.sum(past_weight, axis=-1, keepdims=True) + jnp.sum(recent_weight, axis=-1, keepdims=True)
    past_weight = lax.optimization_barrier((past_weight / denominator).astype(jnp.bfloat16)).astype(jnp.float32)
    recent_weight = lax.optimization_barrier((recent_weight / denominator).astype(jnp.bfloat16)).astype(jnp.float32)
    blended = jnp.einsum("snhgl,lhe->snhge", past_weight, past_values)
    blended = blended + jnp.einsum("snhgm,smhe->snhge", recent_weight, recent_values.astype(jnp.float32))
    return blended.astype(jnp.bfloat16)


def reference(prompt_hidden, kv_weight, kv_bias, new_query, new_kv, decode_prompt, sample_counts, page_table):
    prefix_pages = lax.map(lambda prompt_rows: prompt_keys(prompt_rows, kv_weight, kv_bias), prompt_hidden)
    group_ids = jnp.arange(N_GROUP, dtype=jnp.int32)

    def decode_group(operands):
        group_id, queries, recent, table_row = operands
        own_prompt = decode_prompt[group_id]
        history = prefix_pages[own_prompt]
        earlier = jnp.sum(jnp.where((group_ids < group_id) & (decode_prompt == own_prompt), 1, 0))
        queries = queries.reshape(DSAMP, NEW, KV_HEADS, Q_PER_KV, HEAD_DIM)
        recent = recent.reshape(DSAMP, NEW, KV_HEADS, 2, HEAD_DIM)
        blended = attend(queries, recent[:, :, :, 0], recent[:, :, :, 1], history.reshape(PLEN, KV_HEADS, 2 * HEAD_DIM))
        sample_ids = earlier * DSAMP + jnp.arange(DSAMP, dtype=jnp.int32)
        alive = sample_ids < sample_counts[own_prompt]
        blended = jnp.where(alive[:, None, None, None, None], blended, jnp.zeros_like(blended))
        cache_rows = jnp.zeros((PAGES, PAGE, KV_HEADS * 2 * HEAD_DIM), jnp.bfloat16)
        cache_rows = cache_rows.at[table_row].set(history.reshape(PAGES, PAGE, KV_HEADS * 2 * HEAD_DIM))
        return blended.reshape(DSAMP, NEW, Q_HEADS * HEAD_DIM), cache_rows

    attention_out, kv_cache = lax.map(decode_group, (group_ids, new_query, new_kv, page_table))
    return (attention_out, kv_cache)
```

```python
import functools

import jax
import jax.numpy as jnp
from jax import lax
from jax.experimental import pallas as pl
from jax.experimental.pallas import tpu as pltpu
from jax.sharding import PartitionSpec as P

KV_HEADS = 8
HEAD_DIM = 128
Q_PER_KV = 8
PAGE = 8
ROPE_BASE = 1000000.0
MEMBERS = ("tp", "fork")
VMEM_LIMIT = 48 * 1024 * 1024


def partners(groups):
    if groups & (groups - 1) == 0:
        return [
            (lambda me, s=s: me ^ s, lambda me, s=s: me ^ s) for s in range(groups - 1, 0, -1)
        ]
    return [
        (lambda me, s=s: (me + s) % groups, lambda me, s=s: (me + groups - s) % groups)
        for s in range(1, groups)
    ]


def project_kernel(groups, ordered, prompt_ref, x_ref, w_ref, b_ref, *rest):
    outs, (acc_ref, cos_ref, sin_ref) = rest[:-3], rest[-3:]
    step = pl.program_id(0)
    prompts, rows, depth = x_ref.shape
    width = w_ref.shape[1]
    me = lax.axis_index("group")
    part = jnp.dot(
        x_ref[...].reshape(prompts * rows, depth),
        w_ref[...],
        preferred_element_type=jnp.float32,
    ).reshape(prompts, rows, width)

    @pl.when(step == 0)
    def _():
        acc_ref[...] = part + b_ref[...][None]
        lane = lax.broadcasted_iota(jnp.int32, (rows, HEAD_DIM), 1)
        half = HEAD_DIM // 2
        index = jnp.where(lane < half, lane, lane - half).astype(jnp.float32)
        frequency = jnp.exp(index * (-2.0 * 13.815510557964274 / HEAD_DIM))
        position = me * rows + lax.broadcasted_iota(jnp.int32, (rows, HEAD_DIM), 0)
        angle = position.astype(jnp.float32) * frequency
        cos_ref[...] = jnp.cos(angle)
        sine = jnp.sin(angle)
        sin_ref[...] = jnp.where(lane < half, -sine, sine)

    @pl.when(step > 0)
    def _():
        acc_ref[...] += part

    @pl.when(step == pl.num_programs(0) - 1)
    def _():
        for at, out in enumerate(outs):
            if ordered:
                goes_to = partners(groups)[at][0](me) if at < groups - 1 else me
                total = acc_ref[prompt_ref[goes_to]]
            else:
                total = acc_ref[at]
            key = total[:, :HEAD_DIM]
            swapped = jnp.concatenate(
                [key[:, HEAD_DIM // 2 :], key[:, : HEAD_DIM // 2]], axis=1
            )
            out[:, :HEAD_DIM] = (key * cos_ref[...] + swapped * sin_ref[...]).astype(out.dtype)
            out[:, HEAD_DIM:] = total[:, HEAD_DIM:].astype(out.dtype)


def project(groups, ordered, decode_prompt, prompt_hidden, kv_weight, kv_bias):
    prompts, rows, depth = prompt_hidden.shape
    width = kv_weight.shape[1]
    tile = 1024
    return pl.pallas_call(
        functools.partial(project_kernel, groups, ordered),
        grid=(depth // tile,),
        in_specs=[
            pl.BlockSpec(memory_space=pltpu.SMEM),
            pl.BlockSpec((prompts, rows, tile), lambda k: (0, 0, k)),
            pl.BlockSpec((tile, width), lambda k: (k, 0)),
            pl.BlockSpec((1, width), lambda k: (0, 0)),
        ],
        out_specs=[pl.BlockSpec((rows, width), lambda k: (0, 0))] * prompts,
        out_shape=[jax.ShapeDtypeStruct((rows, width), jnp.bfloat16)] * prompts,
        scratch_shapes=[
            pltpu.VMEM((prompts, rows, width), jnp.float32),
            pltpu.VMEM((rows, HEAD_DIM), jnp.float32),
            pltpu.VMEM((rows, HEAD_DIM), jnp.float32),
        ],
        compiler_params=pltpu.CompilerParams(vmem_limit_bytes=VMEM_LIMIT),
        name="project",
    )(decode_prompt, prompt_hidden, kv_weight, kv_bias.reshape(1, width))


def attend_kernel(groups, steps, prompt_ref, count_ref, table_ref, recent_ref, *rest):
    blocks, out_ref, cache_ref, sem = rest[:groups], rest[groups], rest[groups + 1], rest[groups + 2]
    me = lax.axis_index("group")
    samples = recent_ref.shape[0]
    pages = blocks[0].shape[0]
    sources = [source(me) for _, source in partners(groups)] + [me]
    for block, source in zip(blocks, sources):

        def place(j, carry, block=block, source=source):
            slot = table_ref[0, source * pages + j]
            pltpu.make_async_copy(block.at[j], cache_ref.at[slot], sem).start()
            return carry

        lax.fori_loop(0, pages, place, 0, unroll=True)

    own_prompt = prompt_ref[me]
    earlier = jnp.int32(0)
    for g in range(groups):
        same = jnp.logical_and(g < me, prompt_ref[g] == own_prompt)
        earlier = earlier + jnp.where(same, 1, 0)
    live = count_ref[own_prompt] - earlier * samples

    q_rows = Q_PER_KV * steps
    rows = samples * q_rows
    scaling = HEAD_DIM ** (-0.5)
    query = recent_ref[:, :q_rows, :].reshape(rows, HEAD_DIM)
    recent = recent_ref[:, q_rows:, :].astype(jnp.float32).reshape(samples * 2 * steps, HEAD_DIM)
    recent_key = recent.astype(jnp.bfloat16)
    recent_value = jnp.concatenate([recent[steps:], recent[:steps]], axis=0).astype(jnp.bfloat16)
    contract = (((1,), (1,)), ((), ()))

    def scored(keys):
        return (
            lax.dot_general(query, keys, contract, preferred_element_type=jnp.float32) * scaling
        )

    recent_score = scored(recent_key)
    row = lax.broadcasted_iota(jnp.int32, recent_score.shape, 0)
    column = lax.broadcasted_iota(jnp.int32, recent_score.shape, 1)
    visible = jnp.logical_and(
        row // q_rows == column // (2 * steps), column % (2 * steps) <= row % steps
    )
    recent_score = jnp.where(visible, recent_score, -jnp.inf)
    flat = [block[...].reshape(pages * PAGE, 2 * HEAD_DIM) for block in blocks]
    scores = [scored(block[:, :HEAD_DIM]) for block in flat]
    highest = jnp.max(recent_score, axis=1, keepdims=True)
    for score in scores:
        highest = jnp.maximum(highest, jnp.max(score, axis=1, keepdims=True))
    recent_weight = jnp.exp(recent_score - highest)
    weights = [jnp.exp(score - highest) for score in scores]
    total = jnp.sum(recent_weight, axis=1, keepdims=True)
    for weight in weights:
        total = total + jnp.sum(weight, axis=1, keepdims=True)
    blended = jnp.dot(
        (recent_weight / total).astype(jnp.bfloat16),
        recent_value,
        preferred_element_type=jnp.float32,
    )
    for weight, block in zip(weights, flat):
        blended = blended + jnp.dot(
            (weight / total).astype(jnp.bfloat16),
            block[:, HEAD_DIM:],
            preferred_element_type=jnp.float32,
        )
    sample = lax.broadcasted_iota(jnp.int32, blended.shape, 0) // q_rows
    blended = jnp.where(sample < live, blended, 0.0)
    out_ref[...] = blended.astype(jnp.bfloat16).reshape(samples, q_rows, HEAD_DIM)
    pltpu.make_async_copy(cache_ref, cache_ref, sem).wait()


def attend(groups, steps, decode_prompt, sample_counts, page_table, recent, blocks):
    samples = recent.shape[0]
    page_count = page_table.shape[1]
    smem = pl.BlockSpec(memory_space=pltpu.SMEM)
    vmem = pl.BlockSpec(memory_space=pltpu.VMEM)
    return pl.pallas_call(
        functools.partial(attend_kernel, groups, steps),
        in_specs=[smem, smem, smem, vmem] + [vmem] * groups,
        out_specs=[vmem, pl.BlockSpec(memory_space=pl.ANY)],
        out_shape=[
            jax.ShapeDtypeStruct((samples, Q_PER_KV * steps, HEAD_DIM), jnp.bfloat16),
            jax.ShapeDtypeStruct((page_count, PAGE, 2 * HEAD_DIM), jnp.bfloat16),
        ],
        scratch_shapes=[pltpu.SemaphoreType.DMA],
        compiler_params=pltpu.CompilerParams(vmem_limit_bytes=VMEM_LIMIT),
        name="attend",
    )(decode_prompt, sample_counts, page_table, recent, *blocks)


def local(
    prompt_hidden, kv_weight, kv_bias, new_query, new_kv, decode_prompt, sample_counts, page_table
):
    prompts, rows, _ = prompt_hidden.shape
    groups = lax.axis_size("group")
    steps = new_query.shape[2]
    me = lax.axis_index("group")
    ordered = groups == prompts

    projected = project(groups, ordered, decode_prompt, prompt_hidden, kv_weight, kv_bias)
    if ordered:
        outgoing, own = projected[:-1], projected[-1]
    else:
        pages = jnp.stack(projected)

        def pages_of(group):
            return lax.dynamic_index_in_dim(pages, decode_prompt[group], 0, keepdims=False)

        outgoing = [pages_of(goes_to(me)) for goes_to, _ in partners(groups)]
        own = pages_of(me)
    blocks = [
        lax.ppermute(block, "group", [(i, goes_to(i)) for i in range(groups)])
        for block, (goes_to, _) in zip(outgoing, partners(groups))
    ]
    blocks = [
        block.reshape(rows // PAGE, PAGE, 2 * HEAD_DIM) for block in blocks + [own]
    ]

    by_head = new_query.reshape(steps, KV_HEADS, Q_PER_KV, HEAD_DIM).transpose(1, 2, 0, 3)
    kv_by_head = new_kv.reshape(steps, KV_HEADS, 2, HEAD_DIM).transpose(1, 2, 0, 3)
    packed = jnp.concatenate(
        [
            by_head.reshape(KV_HEADS, Q_PER_KV * steps, HEAD_DIM),
            kv_by_head.reshape(KV_HEADS, 2 * steps, HEAD_DIM),
        ],
        axis=1,
    )
    recent = lax.all_to_all(packed, MEMBERS, 0, 0)

    blended, cache = attend(
        groups, steps, decode_prompt, sample_counts, page_table, recent, blocks
    )
    returned = lax.all_to_all(blended, MEMBERS, 0, 0)
    attention_out = returned.reshape(KV_HEADS * Q_PER_KV, steps, HEAD_DIM).transpose(1, 0, 2)
    return attention_out.reshape(new_query.shape), cache[None]


def solution(mesh):
    return jax.shard_map(
        local,
        mesh=mesh,
        in_specs=(
            P(None, "group", None),
            P(None, MEMBERS),
            P(MEMBERS),
            P("group", MEMBERS, None, None),
            P("group", MEMBERS, None, None),
            P(),
            P(),
            P("group", None),
        ),
        out_specs=(P("group", MEMBERS, None, None), P("group", None, None, MEMBERS)),
        check_vma=False,
    )
```

```python
import functools
import math

import jax
import jax.numpy as jnp
from jax import lax
from jax.experimental import pallas as pl
from jax.experimental.pallas import tpu as pltpu
from jax.sharding import PartitionSpec as P

KV_HEADS = 8
HEAD_DIM = 128
Q_PER_KV = 8
PAGE = 8
ROPE_BASE = 1000000.0
MEMBERS = ("tp", "fork")
CHUNK = 1024
PROJECT_VMEM = 62 * 1024 * 1024
VMEM_LIMIT = 48 * 1024 * 1024
PACK_VMEM = 4 * 1024 * 1024
HIDE_FLOPS = 20 * 10**9


def partners(groups):
    if groups & (groups - 1) == 0:
        return [
            (lambda me, s=s: me ^ s, lambda me, s=s: me ^ s) for s in range(groups - 1, 0, -1)
        ]
    return [
        (lambda me, s=s: (me + s) % groups, lambda me, s=s: (me + groups - s) % groups)
        for s in range(1, groups)
    ]


def project_kernel(
    groups,
    ordered,
    prompt_hbm,
    x_hbm,
    w_hbm,
    b_hbm,
    query_hbm,
    recent_hbm,
    *rest,
):
    outs, packed_hbm, rest = rest[: x_hbm.shape[0]], rest[x_hbm.shape[0]], rest[x_hbm.shape[0] + 1 :]
    prompt_ref, b_ref, query_ref, recent_ref, packed_ref, x_ref, w_ref, total_ref, out_ref = rest[:9]
    small_sem, x_sem, w_sem, out_sem, packed_sem = rest[9:]
    chunks, prompts, rows, depth = x_ref.shape
    small = [
        pltpu.make_async_copy(source, target, small_sem.at[at])
        for at, (source, target) in enumerate(
            [
                (prompt_hbm, prompt_ref),
                (b_hbm, b_ref),
                (recent_hbm, recent_ref),
                (query_hbm, query_ref),
            ]
        )
    ]

    def large(at):
        begin = pl.multiple_of(at * depth, depth)
        return (
            pltpu.make_async_copy(w_hbm.at[pl.ds(begin, depth)], w_ref.at[at], w_sem.at[at]),
            pltpu.make_async_copy(x_hbm.at[:, :, pl.ds(begin, depth)], x_ref.at[at], x_sem.at[at]),
        )

    for copy in small:
        copy.start()
    for at in range(chunks):
        for copy in large(at):
            copy.start()

    me = lax.axis_index("group")
    half = HEAD_DIM // 2
    lane = lax.broadcasted_iota(jnp.int32, (rows, HEAD_DIM), 1)
    index = jnp.where(lane < half, lane, lane - half).astype(jnp.float32)
    frequency = jnp.exp(index * (-2.0 * math.log(ROPE_BASE) / HEAD_DIM))
    position = me * rows + lax.broadcasted_iota(jnp.int32, (rows, HEAD_DIM), 0)
    angle = position.astype(jnp.float32) * frequency
    cosine = jnp.cos(angle)
    sine = jnp.sin(angle)
    sine = jnp.where(lane < half, -sine, sine)
    total_ref[...] = jnp.zeros_like(total_ref)

    def accumulate(at, carry):
        for copy in large(at):
            copy.wait()
        part = jnp.dot(
            x_ref[at].reshape(prompts * rows, depth),
            w_ref[at],
            preferred_element_type=jnp.float32,
        )
        total_ref[...] += part.reshape(total_ref.shape)
        return carry

    early = chunks - chunks // 4
    lax.fori_loop(0, early, accumulate, 0)
    for copy in small:
        copy.wait()
    q_rows = query_ref.shape[1]
    packed_ref[:, :q_rows, :] = query_ref[...]
    packed_ref[:, q_rows:, :] = recent_ref[...]
    pack = pltpu.make_async_copy(packed_ref, packed_hbm, packed_sem)
    pack.start()
    lax.fori_loop(early, chunks, accumulate, 0)
    for at, out in enumerate(outs):
        prompt = at
        if ordered:
            prompt = prompt_ref[partners(groups)[at][0](me) if at < groups - 1 else me]
        total = total_ref[prompt] + b_ref[...]
        key = total[:, :HEAD_DIM]
        swapped = jnp.concatenate([key[:, half:], key[:, :half]], axis=1)
        out_ref[at, :, :HEAD_DIM] = (key * cosine + swapped * sine).astype(out.dtype)
        out_ref[at, :, HEAD_DIM:] = total[:, HEAD_DIM:].astype(out.dtype)
        pltpu.make_async_copy(out_ref.at[at], out, out_sem.at[at]).start()
    pack.wait()
    for at, out in enumerate(outs):
        pltpu.make_async_copy(out_ref.at[at], out, out_sem.at[at]).wait()


def project(groups, ordered, decode_prompt, prompt_hidden, kv_weight, kv_bias, query, recent):
    prompts, rows, depth = prompt_hidden.shape
    width = kv_weight.shape[1]
    chunks = depth // CHUNK
    packed_shape = (query.shape[0], query.shape[1] + recent.shape[1], HEAD_DIM)
    anywhere = pl.BlockSpec(memory_space=pl.ANY)
    return pl.pallas_call(
        functools.partial(project_kernel, groups, ordered),
        in_specs=[anywhere] * 6,
        out_specs=[anywhere] * (prompts + 1),
        out_shape=[jax.ShapeDtypeStruct((rows, width), jnp.bfloat16)] * prompts
        + [jax.ShapeDtypeStruct(packed_shape, query.dtype)],
        scratch_shapes=[
            pltpu.SMEM(decode_prompt.shape, jnp.int32),
            pltpu.VMEM((1, width), jnp.float32),
            pltpu.VMEM(query.shape, query.dtype),
            pltpu.VMEM(recent.shape, recent.dtype),
            pltpu.VMEM(packed_shape, query.dtype),
            pltpu.VMEM((chunks, prompts, rows, CHUNK), jnp.bfloat16),
            pltpu.VMEM((chunks, CHUNK, width), jnp.bfloat16),
            pltpu.VMEM((prompts, rows, width), jnp.float32),
            pltpu.VMEM((prompts, rows, width), jnp.bfloat16),
            pltpu.SemaphoreType.DMA((4,)),
            pltpu.SemaphoreType.DMA((chunks,)),
            pltpu.SemaphoreType.DMA((chunks,)),
            pltpu.SemaphoreType.DMA((prompts,)),
            pltpu.SemaphoreType.DMA,
        ],
        compiler_params=pltpu.CompilerParams(vmem_limit_bytes=PROJECT_VMEM),
        name="project",
    )(decode_prompt, prompt_hidden, kv_weight, kv_bias.reshape(1, width), query, recent)


def store_kernel(groups, table_ref, *rest):
    blocks, (cache_ref, sem) = rest[:groups], rest[groups:]
    me = lax.axis_index("group")
    pages = blocks[0].shape[0]
    sources = [source(me) for _, source in partners(groups)] + [me]
    for block, source in zip(blocks, sources):

        def place(j, carry, block=block, source=source):
            slot = table_ref[0, source * pages + j]
            pltpu.make_async_copy(block.at[j], cache_ref.at[slot], sem).start()
            return carry

        lax.fori_loop(0, pages, place, 0, unroll=True)
    pltpu.make_async_copy(cache_ref, cache_ref, sem).wait()


def store(groups, page_table, blocks):
    return pl.pallas_call(
        functools.partial(store_kernel, groups),
        in_specs=[pl.BlockSpec(memory_space=pltpu.SMEM)]
        + [pl.BlockSpec(memory_space=pltpu.VMEM)] * groups,
        out_specs=pl.BlockSpec(memory_space=pl.ANY),
        out_shape=jax.ShapeDtypeStruct((page_table.shape[1],) + blocks[0].shape[1:], jnp.bfloat16),
        scratch_shapes=[pltpu.SemaphoreType.DMA],
        cost_estimate=pl.CostEstimate(flops=HIDE_FLOPS, transcendentals=0, bytes_accessed=0),
        compiler_params=pltpu.CompilerParams(vmem_limit_bytes=PACK_VMEM),
        name="store",
    )(page_table, *blocks)


def attend_kernel(groups, steps, prompt_ref, count_ref, cache_ref, recent_ref, *rest):
    del cache_ref
    blocks, out_ref = rest[:groups], rest[groups]
    me = lax.axis_index("group")
    samples = recent_ref.shape[0]
    pages = blocks[0].shape[0]
    own_prompt = prompt_ref[me]
    earlier = jnp.int32(0)
    for g in range(groups):
        same = jnp.logical_and(g < me, prompt_ref[g] == own_prompt)
        earlier = earlier + jnp.where(same, 1, 0)
    live = count_ref[own_prompt] - earlier * samples

    q_rows = Q_PER_KV * steps
    rows = samples * q_rows
    scaling = HEAD_DIM ** (-0.5)
    query = recent_ref[:, :q_rows, :].reshape(rows, HEAD_DIM)
    recent = recent_ref[:, q_rows:, :].astype(jnp.float32).reshape(samples * 2 * steps, HEAD_DIM)
    recent_key = recent.astype(jnp.bfloat16)
    recent_value = jnp.concatenate([recent[steps:], recent[:steps]], axis=0).astype(jnp.bfloat16)
    contract = (((1,), (1,)), ((), ()))

    def scored(keys):
        return (
            lax.dot_general(query, keys, contract, preferred_element_type=jnp.float32) * scaling
        )

    recent_score = scored(recent_key)
    row = lax.broadcasted_iota(jnp.int32, recent_score.shape, 0)
    column = lax.broadcasted_iota(jnp.int32, recent_score.shape, 1)
    visible = jnp.logical_and(
        row // q_rows == column // (2 * steps), column % (2 * steps) <= row % steps
    )
    recent_score = jnp.where(visible, recent_score, -jnp.inf)
    flat = [block[...].reshape(pages * PAGE, 2 * HEAD_DIM) for block in blocks]
    scores = [scored(block[:, :HEAD_DIM]) for block in flat]
    highest = jnp.max(recent_score, axis=1, keepdims=True)
    for score in scores:
        highest = jnp.maximum(highest, jnp.max(score, axis=1, keepdims=True))
    recent_weight = jnp.exp(recent_score - highest)
    weights = [jnp.exp(score - highest) for score in scores]
    total = jnp.sum(recent_weight, axis=1, keepdims=True)
    for weight in weights:
        total = total + jnp.sum(weight, axis=1, keepdims=True)
    blended = jnp.dot(
        (recent_weight / total).astype(jnp.bfloat16),
        recent_value,
        preferred_element_type=jnp.float32,
    )
    for weight, block in zip(weights, flat):
        blended = blended + jnp.dot(
            (weight / total).astype(jnp.bfloat16),
            block[:, HEAD_DIM:],
            preferred_element_type=jnp.float32,
        )
    sample = lax.broadcasted_iota(jnp.int32, blended.shape, 0) // q_rows
    blended = jnp.where(sample < live, blended, 0.0)
    out_ref[...] = blended.astype(jnp.bfloat16).reshape(samples, q_rows, HEAD_DIM)


def attend(groups, steps, decode_prompt, sample_counts, cache, recent, blocks):
    samples = recent.shape[0]
    smem = pl.BlockSpec(memory_space=pltpu.SMEM)
    vmem = pl.BlockSpec(memory_space=pltpu.VMEM)
    return pl.pallas_call(
        functools.partial(attend_kernel, groups, steps),
        in_specs=[smem, smem, pl.BlockSpec(memory_space=pl.ANY), vmem] + [vmem] * groups,
        out_specs=vmem,
        out_shape=jax.ShapeDtypeStruct((samples, Q_PER_KV * steps, HEAD_DIM), jnp.bfloat16),
        compiler_params=pltpu.CompilerParams(vmem_limit_bytes=VMEM_LIMIT),
        name="attend",
    )(decode_prompt, sample_counts, cache, recent, *blocks)


def local(
    prompt_hidden, kv_weight, kv_bias, new_query, new_kv, decode_prompt, sample_counts, page_table
):
    prompts, rows, _ = prompt_hidden.shape
    groups = lax.axis_size("group")
    steps = new_query.shape[2]
    me = lax.axis_index("group")
    ordered = groups == prompts

    by_head = new_query.reshape(steps, KV_HEADS, Q_PER_KV, HEAD_DIM).transpose(1, 2, 0, 3)
    kv_by_head = new_kv.reshape(steps, KV_HEADS, 2, HEAD_DIM).transpose(1, 2, 0, 3)
    *projected, packed = project(
        groups,
        ordered,
        decode_prompt,
        prompt_hidden,
        kv_weight,
        kv_bias,
        by_head.reshape(KV_HEADS, Q_PER_KV * steps, HEAD_DIM),
        kv_by_head.reshape(KV_HEADS, 2 * steps, HEAD_DIM),
    )
    if ordered:
        outgoing, own = projected[:-1], projected[-1]
    else:
        pages = jnp.stack(projected)

        def pages_of(group):
            return lax.dynamic_index_in_dim(pages, decode_prompt[group], 0, keepdims=False)

        outgoing = [pages_of(goes_to(me)) for goes_to, _ in partners(groups)]
        own = pages_of(me)
    blocks = [
        lax.ppermute(block, "group", [(i, goes_to(i)) for i in range(groups)])
        for block, (goes_to, _) in zip(outgoing, partners(groups))
    ]
    blocks = [
        block.reshape(rows // PAGE, PAGE, 2 * HEAD_DIM) for block in blocks + [own]
    ]

    recent = lax.all_to_all(packed, MEMBERS, 0, 0)

    cache = store(groups, page_table, blocks)
    blended = attend(groups, steps, decode_prompt, sample_counts, cache, recent, blocks)
    returned = lax.all_to_all(blended, MEMBERS, 0, 0)
    attention_out = returned.reshape(KV_HEADS * Q_PER_KV, steps, HEAD_DIM).transpose(1, 0, 2)
    return attention_out.reshape(new_query.shape), cache[None]


def solution(mesh):
    return jax.shard_map(
        local,
        mesh=mesh,
        in_specs=(
            P(None, "group", None),
            P(None, MEMBERS),
            P(MEMBERS),
            P("group", MEMBERS, None, None),
            P("group", MEMBERS, None, None),
            P(),
            P(),
            P("group", None),
        ),
        out_specs=(P("group", MEMBERS, None, None), P("group", None, None, MEMBERS)),
        check_vma=False,
    )
```

```python
import functools
import math

import jax
import jax.numpy as jnp
from jax import lax
from jax.experimental import pallas as pl
from jax.experimental.pallas import tpu as pltpu
from jax.sharding import PartitionSpec as P

KV_HEADS = 8
HEAD_DIM = 128
Q_PER_KV = 8
PAGE = 8
ROPE_BASE = 1000000.0
MEMBERS = ("tp", "fork")
CHUNK = 1024
VMEM_LIMIT = 40 * 1024 * 1024
PACK_VMEM = 4 * 1024 * 1024
HIDE_FLOPS = 20 * 10**9


def partners(groups):
    if groups & (groups - 1) == 0:
        return [
            (lambda me, s=s: me ^ s, lambda me, s=s: me ^ s) for s in range(groups - 1, 0, -1)
        ]
    return [
        (lambda me, s=s: (me + s) % groups, lambda me, s=s: (me + groups - s) % groups)
        for s in range(1, groups)
    ]


def in_hbm(array):
    return pltpu.with_memory_space_constraint(array, pltpu.HBM)


def project_kernel(
    groups,
    ordered,
    prompt_hbm,
    x_hbm,
    w_hbm,
    b_hbm,
    query_hbm,
    recent_hbm,
    *rest,
):
    outs, packed_ref, rest = rest[: x_hbm.shape[0]], rest[x_hbm.shape[0]], rest[x_hbm.shape[0] + 1 :]
    prompt_ref, b_ref, query_ref, recent_ref, x_ref, w_ref, total_ref = rest[:7]
    small_sem, x_sem, w_sem = rest[7:]
    chunks, prompts, rows, depth = x_ref.shape
    small = [
        pltpu.make_async_copy(source, target, small_sem.at[at])
        for at, (source, target) in enumerate(
            [
                (prompt_hbm, prompt_ref),
                (b_hbm, b_ref),
                (recent_hbm, recent_ref),
                (query_hbm, query_ref),
            ]
        )
    ]

    def large(at):
        begin = pl.multiple_of(at * depth, depth)
        return (
            pltpu.make_async_copy(w_hbm.at[pl.ds(begin, depth)], w_ref.at[at], w_sem.at[at]),
            pltpu.make_async_copy(x_hbm.at[:, :, pl.ds(begin, depth)], x_ref.at[at], x_sem.at[at]),
        )

    for copy in small:
        copy.start()
    for at in range(chunks):
        for copy in large(at):
            copy.start()

    me = lax.axis_index("group")
    half = HEAD_DIM // 2
    lane = lax.broadcasted_iota(jnp.int32, (rows, HEAD_DIM), 1)
    index = jnp.where(lane < half, lane, lane - half).astype(jnp.float32)
    frequency = jnp.exp(index * (-2.0 * math.log(ROPE_BASE) / HEAD_DIM))
    position = me * rows + lax.broadcasted_iota(jnp.int32, (rows, HEAD_DIM), 0)
    angle = position.astype(jnp.float32) * frequency
    cosine = jnp.cos(angle)
    sine = jnp.sin(angle)
    sine = jnp.where(lane < half, -sine, sine)
    total_ref[...] = jnp.zeros_like(total_ref)

    def accumulate(at, carry):
        for copy in large(at):
            copy.wait()
        part = jnp.dot(
            x_ref[at].reshape(prompts * rows, depth),
            w_ref[at],
            preferred_element_type=jnp.float32,
        )
        total_ref[...] += part.reshape(total_ref.shape)
        return carry

    early = chunks - chunks // 4
    lax.fori_loop(0, early, accumulate, 0)
    for copy in small:
        copy.wait()
    q_rows = query_ref.shape[1]
    packed_ref[:, :q_rows, :] = query_ref[...]
    packed_ref[:, q_rows:, :] = recent_ref[...]
    lax.fori_loop(early, chunks, accumulate, 0)
    for at, out in enumerate(outs):
        prompt = at
        if ordered:
            prompt = prompt_ref[partners(groups)[at][0](me) if at < groups - 1 else me]
        total = total_ref[prompt] + b_ref[...]
        key = total[:, :HEAD_DIM]
        swapped = jnp.concatenate([key[:, half:], key[:, :half]], axis=1)
        out[:, :HEAD_DIM] = (key * cosine + swapped * sine).astype(out.dtype)
        out[:, HEAD_DIM:] = total[:, HEAD_DIM:].astype(out.dtype)


def project(groups, ordered, decode_prompt, prompt_hidden, kv_weight, kv_bias, query, recent):
    prompts, rows, depth = prompt_hidden.shape
    width = kv_weight.shape[1]
    chunks = depth // CHUNK
    packed_shape = (query.shape[0], query.shape[1] + recent.shape[1], HEAD_DIM)
    operands = (decode_prompt, prompt_hidden, kv_weight, kv_bias.reshape(1, width), query, recent)
    return pl.pallas_call(
        functools.partial(project_kernel, groups, ordered),
        in_specs=[pl.BlockSpec(memory_space=pl.ANY)] * len(operands),
        out_specs=[pl.BlockSpec(memory_space=pltpu.VMEM)] * (prompts + 1),
        out_shape=[pltpu.VMEM((rows, width), jnp.bfloat16)] * prompts
        + [pltpu.VMEM(packed_shape, query.dtype)],
        scratch_shapes=[
            pltpu.SMEM(decode_prompt.shape, jnp.int32),
            pltpu.VMEM((1, width), jnp.float32),
            pltpu.VMEM(query.shape, query.dtype),
            pltpu.VMEM(recent.shape, recent.dtype),
            pltpu.VMEM((chunks, prompts, rows, CHUNK), jnp.bfloat16),
            pltpu.VMEM((chunks, CHUNK, width), jnp.bfloat16),
            pltpu.VMEM((prompts, rows, width), jnp.float32),
            pltpu.SemaphoreType.DMA((4,)),
            pltpu.SemaphoreType.DMA((chunks,)),
            pltpu.SemaphoreType.DMA((chunks,)),
        ],
        compiler_params=pltpu.CompilerParams(vmem_limit_bytes=VMEM_LIMIT),
        name="project",
    )(*map(in_hbm, operands))


def store_kernel(groups, table_ref, *rest):
    blocks, (cache_ref, sem) = rest[:groups], rest[groups:]
    me = lax.axis_index("group")
    pages = blocks[0].shape[0]
    sources = [source(me) for _, source in partners(groups)] + [me]
    for block, source in zip(blocks, sources):

        def place(j, carry, block=block, source=source):
            slot = table_ref[0, source * pages + j]
            pltpu.make_async_copy(block.at[j], cache_ref.at[slot], sem).start()
            return carry

        lax.fori_loop(0, pages, place, 0, unroll=True)
    pltpu.make_async_copy(cache_ref, cache_ref, sem).wait()


def store(groups, page_table, blocks):
    return pl.pallas_call(
        functools.partial(store_kernel, groups),
        in_specs=[pl.BlockSpec(memory_space=pltpu.SMEM)]
        + [pl.BlockSpec(memory_space=pltpu.VMEM)] * groups,
        out_specs=pl.BlockSpec(memory_space=pl.ANY),
        out_shape=jax.ShapeDtypeStruct((page_table.shape[1],) + blocks[0].shape[1:], jnp.bfloat16),
        scratch_shapes=[pltpu.SemaphoreType.DMA],
        cost_estimate=pl.CostEstimate(flops=HIDE_FLOPS, transcendentals=0, bytes_accessed=0),
        compiler_params=pltpu.CompilerParams(vmem_limit_bytes=PACK_VMEM),
        name="store",
    )(page_table, *blocks)


def attend_kernel(groups, steps, prompt_ref, count_ref, cache_ref, recent_ref, *rest):
    del cache_ref
    blocks, out_ref = rest[:groups], rest[groups]
    me = lax.axis_index("group")
    samples = recent_ref.shape[0]
    pages = blocks[0].shape[0]
    own_prompt = prompt_ref[me]
    earlier = jnp.int32(0)
    for g in range(groups):
        same = jnp.logical_and(g < me, prompt_ref[g] == own_prompt)
        earlier = earlier + jnp.where(same, 1, 0)
    live = count_ref[own_prompt] - earlier * samples

    q_rows = Q_PER_KV * steps
    rows = samples * q_rows
    scaling = HEAD_DIM ** (-0.5)
    query = recent_ref[:, :q_rows, :].reshape(rows, HEAD_DIM)
    recent = recent_ref[:, q_rows:, :].astype(jnp.float32).reshape(samples * 2 * steps, HEAD_DIM)
    recent_key = recent.astype(jnp.bfloat16)
    recent_value = jnp.concatenate([recent[steps:], recent[:steps]], axis=0).astype(jnp.bfloat16)
    contract = (((1,), (1,)), ((), ()))

    def scored(keys):
        return (
            lax.dot_general(query, keys, contract, preferred_element_type=jnp.float32) * scaling
        )

    recent_score = scored(recent_key)
    row = lax.broadcasted_iota(jnp.int32, recent_score.shape, 0)
    column = lax.broadcasted_iota(jnp.int32, recent_score.shape, 1)
    visible = jnp.logical_and(
        row // q_rows == column // (2 * steps), column % (2 * steps) <= row % steps
    )
    recent_score = jnp.where(visible, recent_score, -jnp.inf)
    flat = [block[...].reshape(pages * PAGE, 2 * HEAD_DIM) for block in blocks]
    scores = [scored(block[:, :HEAD_DIM]) for block in flat]
    highest = jnp.max(recent_score, axis=1, keepdims=True)
    for score in scores:
        highest = jnp.maximum(highest, jnp.max(score, axis=1, keepdims=True))
    recent_weight = jnp.exp(recent_score - highest)
    weights = [jnp.exp(score - highest) for score in scores]
    total = jnp.sum(recent_weight, axis=1, keepdims=True)
    for weight in weights:
        total = total + jnp.sum(weight, axis=1, keepdims=True)
    blended = jnp.dot(
        (recent_weight / total).astype(jnp.bfloat16),
        recent_value,
        preferred_element_type=jnp.float32,
    )
    for weight, block in zip(weights, flat):
        blended = blended + jnp.dot(
            (weight / total).astype(jnp.bfloat16),
            block[:, HEAD_DIM:],
            preferred_element_type=jnp.float32,
        )
    sample = lax.broadcasted_iota(jnp.int32, blended.shape, 0) // q_rows
    blended = jnp.where(sample < live, blended, 0.0)
    out_ref[...] = blended.astype(jnp.bfloat16).reshape(samples, q_rows, HEAD_DIM)


def attend(groups, steps, decode_prompt, sample_counts, cache, recent, blocks):
    samples = recent.shape[0]
    smem = pl.BlockSpec(memory_space=pltpu.SMEM)
    vmem = pl.BlockSpec(memory_space=pltpu.VMEM)
    return pl.pallas_call(
        functools.partial(attend_kernel, groups, steps),
        in_specs=[smem, smem, pl.BlockSpec(memory_space=pl.ANY), vmem] + [vmem] * groups,
        out_specs=vmem,
        out_shape=jax.ShapeDtypeStruct((samples, Q_PER_KV * steps, HEAD_DIM), jnp.bfloat16),
        compiler_params=pltpu.CompilerParams(vmem_limit_bytes=VMEM_LIMIT),
        name="attend",
    )(decode_prompt, sample_counts, in_hbm(cache), recent, *blocks)


def local(
    prompt_hidden, kv_weight, kv_bias, new_query, new_kv, decode_prompt, sample_counts, page_table
):
    prompts, rows, _ = prompt_hidden.shape
    groups = lax.axis_size("group")
    steps = new_query.shape[2]
    me = lax.axis_index("group")
    ordered = groups == prompts

    by_head = new_query.reshape(steps, KV_HEADS, Q_PER_KV, HEAD_DIM).transpose(1, 2, 0, 3)
    kv_by_head = new_kv.reshape(steps, KV_HEADS, 2, HEAD_DIM).transpose(1, 2, 0, 3)
    *projected, packed = project(
        groups,
        ordered,
        decode_prompt,
        prompt_hidden,
        kv_weight,
        kv_bias,
        by_head.reshape(KV_HEADS, Q_PER_KV * steps, HEAD_DIM),
        kv_by_head.reshape(KV_HEADS, 2 * steps, HEAD_DIM),
    )
    if ordered:
        outgoing, own = projected[:-1], projected[-1]
    else:
        pages = jnp.stack(projected)

        def pages_of(group):
            return lax.dynamic_index_in_dim(pages, decode_prompt[group], 0, keepdims=False)

        outgoing = [pages_of(goes_to(me)) for goes_to, _ in partners(groups)]
        own = pages_of(me)
    blocks = [
        lax.ppermute(block, "group", [(i, goes_to(i)) for i in range(groups)])
        for block, (goes_to, _) in zip(outgoing, partners(groups))
    ]
    blocks = [
        block.reshape(rows // PAGE, PAGE, 2 * HEAD_DIM) for block in blocks + [own]
    ]

    recent = lax.all_to_all(packed, MEMBERS, 0, 0)

    cache = store(groups, page_table, blocks)
    blended = attend(groups, steps, decode_prompt, sample_counts, cache, recent, blocks)
    returned = lax.all_to_all(blended, MEMBERS, 0, 0)
    attention_out = returned.reshape(KV_HEADS * Q_PER_KV, steps, HEAD_DIM).transpose(1, 0, 2)
    return attention_out.reshape(new_query.shape), cache[None]


def solution(mesh):
    return jax.shard_map(
        local,
        mesh=mesh,
        in_specs=(
            P(None, "group", None),
            P(None, MEMBERS),
            P(MEMBERS),
            P("group", MEMBERS, None, None),
            P("group", MEMBERS, None, None),
            P(),
            P(),
            P("group", None),
        ),
        out_specs=(P("group", MEMBERS, None, None), P("group", None, None, MEMBERS)),
        check_vma=False,
    )
```

```python
import functools
import math

import jax
import jax.numpy as jnp
from jax import lax
from jax.experimental import pallas as pl
from jax.experimental.pallas import tpu as pltpu
from jax.sharding import PartitionSpec as P

KV_HEADS = 8
HEAD_DIM = 128
Q_PER_KV = 8
PAGE = 8
ROPE_BASE = 1000000.0
MEMBERS = ("tp", "fork")
CHUNK = 1024
VMEM_LIMIT = 40 * 1024 * 1024
PACK_VMEM = 4 * 1024 * 1024
HIDE_FLOPS = 20 * 10**9


def partners(groups):
    if groups & (groups - 1) == 0:
        return [
            (lambda me, s=s: me ^ s, lambda me, s=s: me ^ s) for s in range(groups - 1, 0, -1)
        ]
    return [
        (lambda me, s=s: (me + s) % groups, lambda me, s=s: (me + groups - s) % groups)
        for s in range(1, groups)
    ]


SIBLING = 2
PEERS = (5, 4, 1)


def in_hbm(array):
    return pltpu.with_memory_space_constraint(array, pltpu.HBM)


def project_kernel(
    groups,
    ordered,
    prompt_hbm,
    count_hbm,
    x_hbm,
    w_hbm,
    b_hbm,
    query_hbm,
    recent_hbm,
    *rest,
):
    prompts = x_hbm.shape[0]
    packets = len(PEERS) + 1
    outs, packed, rest = rest[:prompts], rest[prompts : prompts + packets], rest[prompts + packets :]
    alive_ref, prompt_ref, count_ref, b_ref, query_ref, recent_ref, x_ref, w_ref, total_ref = rest[:9]
    small_sem, x_sem, w_sem = rest[9:]
    chunks, prompts, rows, depth = x_ref.shape
    small = [
        pltpu.make_async_copy(source, target, small_sem.at[at])
        for at, (source, target) in enumerate(
            [
                (prompt_hbm, prompt_ref),
                (count_hbm, count_ref),
                (b_hbm, b_ref),
                (recent_hbm, recent_ref),
                (query_hbm, query_ref),
            ]
        )
    ]

    def large(at):
        begin = pl.multiple_of(at * depth, depth)
        return (
            pltpu.make_async_copy(w_hbm.at[pl.ds(begin, depth)], w_ref.at[at], w_sem.at[at]),
            pltpu.make_async_copy(x_hbm.at[:, :, pl.ds(begin, depth)], x_ref.at[at], x_sem.at[at]),
        )

    for copy in small:
        copy.start()
    for at in range(chunks):
        for copy in large(at):
            copy.start()

    me = lax.axis_index("group")
    half = HEAD_DIM // 2
    lane = lax.broadcasted_iota(jnp.int32, (rows, HEAD_DIM), 1)
    index = jnp.where(lane < half, lane, lane - half).astype(jnp.float32)
    frequency = jnp.exp(index * (-2.0 * math.log(ROPE_BASE) / HEAD_DIM))
    position = me * rows + lax.broadcasted_iota(jnp.int32, (rows, HEAD_DIM), 0)
    angle = position.astype(jnp.float32) * frequency
    cosine = jnp.cos(angle)
    sine = jnp.sin(angle)
    sine = jnp.where(lane < half, -sine, sine)
    total_ref[...] = jnp.zeros_like(total_ref)

    def accumulate(at, carry):
        for copy in large(at):
            copy.wait()
        part = jnp.dot(
            x_ref[at].reshape(prompts * rows, depth),
            w_ref[at],
            preferred_element_type=jnp.float32,
        )
        total_ref[...] += part.reshape(total_ref.shape)
        return carry

    early = chunks - chunks // 4
    lax.fori_loop(0, early, accumulate, 0)
    for copy in small:
        copy.wait()
    q_rows = query_ref.shape[1]
    member = lax.axis_index(MEMBERS)
    for distance, packet in zip(PEERS + (0,), packed):
        for at in range(2):
            head = member ^ distance ^ (SIBLING * at)
            packet[at, :q_rows, :] = query_ref[head]
            packet[at, q_rows:, :] = recent_ref[head]
    own_prompt = prompt_ref[me]
    earlier = jnp.int32(0)
    for g in range(groups):
        same = jnp.logical_and(g < me, prompt_ref[g] == own_prompt)
        earlier = earlier + jnp.where(same, 1, 0)
    limit = count_ref[own_prompt] - earlier * lax.axis_size(MEMBERS)
    for at, distance in enumerate(PEERS + (0,)):
        live = jnp.where((member ^ distance) < limit, 1.0, 0.0)
        alive_ref[at * q_rows : (at + 1) * q_rows, :] = jnp.full((q_rows, HEAD_DIM), live)
    lax.fori_loop(early, chunks, accumulate, 0)
    for at, out in enumerate(outs):
        prompt = at
        if ordered:
            prompt = prompt_ref[partners(groups)[at][0](me) if at < groups - 1 else me]
        total = total_ref[prompt] + b_ref[...]
        key = total[:, :HEAD_DIM]
        swapped = jnp.concatenate([key[:, half:], key[:, :half]], axis=1)
        out[:, :HEAD_DIM] = (key * cosine + swapped * sine).astype(out.dtype)
        out[:, HEAD_DIM:] = total[:, HEAD_DIM:].astype(out.dtype)


def project(groups, ordered, decode_prompt, sample_counts, prompt_hidden, kv_weight, kv_bias, query, recent):
    prompts, rows, depth = prompt_hidden.shape
    width = kv_weight.shape[1]
    chunks = depth // CHUNK
    packet = pltpu.VMEM((2, query.shape[1] + recent.shape[1], HEAD_DIM), query.dtype)
    packets = [packet] * (len(PEERS) + 1)
    alive = pltpu.VMEM((len(packets) * query.shape[1], HEAD_DIM), jnp.float32)
    bias = kv_bias.reshape(1, width)
    operands = (decode_prompt, sample_counts, prompt_hidden, kv_weight, bias, query, recent)
    return pl.pallas_call(
        functools.partial(project_kernel, groups, ordered),
        in_specs=[pl.BlockSpec(memory_space=pl.ANY)] * len(operands),
        out_specs=[pl.BlockSpec(memory_space=pltpu.VMEM)] * (prompts + len(packets) + 1),
        out_shape=[pltpu.VMEM((rows, width), jnp.bfloat16)] * prompts + packets + [alive],
        scratch_shapes=[
            pltpu.SMEM(decode_prompt.shape, jnp.int32),
            pltpu.SMEM(sample_counts.shape, jnp.int32),
            pltpu.VMEM((1, width), jnp.float32),
            pltpu.VMEM(query.shape, query.dtype),
            pltpu.VMEM(recent.shape, recent.dtype),
            pltpu.VMEM((chunks, prompts, rows, CHUNK), jnp.bfloat16),
            pltpu.VMEM((chunks, CHUNK, width), jnp.bfloat16),
            pltpu.VMEM((prompts, rows, width), jnp.float32),
            pltpu.SemaphoreType.DMA((5,)),
            pltpu.SemaphoreType.DMA((chunks,)),
            pltpu.SemaphoreType.DMA((chunks,)),
        ],
        compiler_params=pltpu.CompilerParams(vmem_limit_bytes=VMEM_LIMIT),
        name="project",
    )(*map(in_hbm, operands))


def store_kernel(groups, table_ref, *rest):
    blocks, (cache_ref, sem) = rest[:groups], rest[groups:]
    me = lax.axis_index("group")
    pages = blocks[0].shape[0]
    sources = [source(me) for _, source in partners(groups)] + [me]
    for block, source in zip(blocks, sources):

        def place(j, carry, block=block, source=source):
            slot = table_ref[0, source * pages + j]
            pltpu.make_async_copy(block.at[j], cache_ref.at[slot], sem).start()
            return carry

        lax.fori_loop(0, pages, place, 0, unroll=True)
    pltpu.make_async_copy(cache_ref, cache_ref, sem).wait()


def store(groups, page_table, blocks):
    return pl.pallas_call(
        functools.partial(store_kernel, groups),
        in_specs=[pl.BlockSpec(memory_space=pltpu.SMEM)]
        + [pl.BlockSpec(memory_space=pltpu.VMEM)] * groups,
        out_specs=pl.BlockSpec(memory_space=pl.ANY),
        out_shape=jax.ShapeDtypeStruct((page_table.shape[1],) + blocks[0].shape[1:], jnp.bfloat16),
        scratch_shapes=[pltpu.SemaphoreType.DMA],
        cost_estimate=pl.CostEstimate(flops=HIDE_FLOPS, transcendentals=0, bytes_accessed=0),
        compiler_params=pltpu.CompilerParams(vmem_limit_bytes=PACK_VMEM),
        name="store",
    )(page_table, *blocks)


def arrange_kernel(steps, *refs):
    packets, (query_ref, key_ref, value_ref) = refs[:-3], refs[-3:]
    q_rows = Q_PER_KV * steps
    for at in range(2):
        recent = jnp.concatenate(
            [packet[at, q_rows:, :].astype(jnp.float32) for packet in packets], axis=0
        )
        shifted = jnp.concatenate([recent[steps:], recent[:steps]], axis=0)
        key_ref[at] = recent.astype(key_ref.dtype)
        value_ref[at] = shifted.astype(value_ref.dtype)
        for sample, packet in enumerate(packets):
            query_ref[at, sample * q_rows : (sample + 1) * q_rows, :] = packet[at, :q_rows, :]


def arrange(steps, packets):
    samples, dtype = len(packets), packets[0].dtype
    vmem = pl.BlockSpec(memory_space=pltpu.VMEM)
    recent = pltpu.VMEM((2, samples * 2 * steps, HEAD_DIM), dtype)
    return pl.pallas_call(
        functools.partial(arrange_kernel, steps),
        in_specs=[vmem] * samples,
        out_specs=[vmem] * 3,
        out_shape=[
            pltpu.VMEM((2, samples * Q_PER_KV * steps, HEAD_DIM), dtype),
            recent,
            recent,
        ],
        cost_estimate=pl.CostEstimate(flops=HIDE_FLOPS, transcendentals=0, bytes_accessed=0),
        compiler_params=pltpu.CompilerParams(vmem_limit_bytes=PACK_VMEM),
        name="arrange",
    )(*packets)


def attend_head(steps, alive, query, recent_key, recent_value, blocks):
    q_rows = Q_PER_KV * steps
    scaling = HEAD_DIM ** (-0.5)
    contract = (((1,), (1,)), ((), ()))

    def scored(keys):
        return (
            lax.dot_general(query, keys, contract, preferred_element_type=jnp.float32) * scaling
        )

    recent_score = scored(recent_key)
    row = lax.broadcasted_iota(jnp.int32, recent_score.shape, 0)
    column = lax.broadcasted_iota(jnp.int32, recent_score.shape, 1)
    visible = jnp.logical_and(
        row // q_rows == column // (2 * steps), column % (2 * steps) <= row % steps
    )
    recent_score = jnp.where(visible, recent_score, -jnp.inf)
    scores = [scored(block[:, :HEAD_DIM]) for block in blocks]
    highest = functools.reduce(jnp.maximum, scores).max(axis=1, keepdims=True)
    highest = jnp.maximum(highest, jnp.max(recent_score, axis=1, keepdims=True))
    recent_weight = jnp.exp(recent_score - highest)
    weights = [jnp.exp(score - highest) for score in scores]
    total = functools.reduce(jnp.add, weights).sum(axis=1, keepdims=True)
    total = total + jnp.sum(recent_weight, axis=1, keepdims=True)
    blended = jnp.dot(
        recent_weight.astype(jnp.bfloat16), recent_value, preferred_element_type=jnp.float32
    )
    for weight, block in zip(weights, blocks):
        blended = blended + jnp.dot(
            weight.astype(jnp.bfloat16), block[:, HEAD_DIM:], preferred_element_type=jnp.float32
        )
    blended = blended / total
    return jnp.where(alive > 0.0, blended, 0.0)


def attend_kernel(groups, steps, alive_ref, *rest):
    arranged, rest = rest[:3], rest[3:]
    head_blocks, outs = (rest[:groups], rest[groups : 2 * groups]), rest[2 * groups :]
    q_rows = Q_PER_KV * steps
    for at, refs in enumerate(head_blocks):
        blended = attend_head(
            steps,
            alive_ref[...],
            *[ref[at] for ref in arranged],
            [block[...] for block in refs],
        ).astype(jnp.bfloat16)
        for to, out in enumerate(outs):
            out[at] = blended[to * q_rows : (to + 1) * q_rows]


def attend(groups, steps, alive, arranged, own_blocks, sibling_blocks):
    packets = len(PEERS) + 1
    vmem = pl.BlockSpec(memory_space=pltpu.VMEM)
    return pl.pallas_call(
        functools.partial(attend_kernel, groups, steps),
        in_specs=[vmem] * (1 + len(arranged) + 2 * groups),
        out_specs=[vmem] * packets,
        out_shape=[pltpu.VMEM((2, Q_PER_KV * steps, HEAD_DIM), jnp.bfloat16)] * packets,
        compiler_params=pltpu.CompilerParams(vmem_limit_bytes=VMEM_LIMIT),
        name="attend",
    )(alive, *arranged, *own_blocks, *sibling_blocks)


def gather_kernel(*refs):
    parts, out_ref, sem = refs[:-2], refs[-2], refs[-1]
    member = lax.axis_index(MEMBERS)
    copies = []
    for distance, part in zip(PEERS + (0,), parts):
        for at in range(2):
            head = member ^ distance ^ (SIBLING * at)
            copies.append(
                pltpu.make_async_copy(part.at[at], out_ref.at[head], sem.at[len(copies)])
            )
    for copy in copies:
        copy.start()
    for copy in copies:
        copy.wait()


def gather(parts):
    heads, rows, width = 2 * len(parts), parts[0].shape[1], parts[0].shape[2]
    return pl.pallas_call(
        gather_kernel,
        in_specs=[pl.BlockSpec(memory_space=pltpu.VMEM)] * len(parts),
        out_specs=pl.BlockSpec(memory_space=pl.ANY),
        out_shape=pltpu.HBM((heads, rows, width), parts[0].dtype),
        scratch_shapes=[pltpu.SemaphoreType.DMA((heads,))],
        compiler_params=pltpu.CompilerParams(vmem_limit_bytes=PACK_VMEM),
        name="gather",
    )(*parts)


def local(
    prompt_hidden, kv_weight, kv_bias, new_query, new_kv, decode_prompt, sample_counts, page_table
):
    prompts, rows, _ = prompt_hidden.shape
    groups = lax.axis_size("group")
    steps = new_query.shape[2]
    me = lax.axis_index("group")
    ordered = groups == prompts

    by_head = new_query.reshape(steps, KV_HEADS, Q_PER_KV, HEAD_DIM).transpose(1, 2, 0, 3)
    kv_by_head = new_kv.reshape(steps, KV_HEADS, 2, HEAD_DIM).transpose(1, 2, 0, 3)
    results = project(
        groups,
        ordered,
        decode_prompt,
        sample_counts,
        prompt_hidden,
        kv_weight,
        kv_bias,
        by_head.reshape(KV_HEADS, Q_PER_KV * steps, HEAD_DIM),
        kv_by_head.reshape(KV_HEADS, 2 * steps, HEAD_DIM),
    )
    projected, packets, alive = results[:prompts], results[prompts:-1], results[-1]
    if ordered:
        outgoing, own = projected[:-1], projected[-1]
    else:
        pages = jnp.stack(projected)

        def pages_of(group):
            return lax.dynamic_index_in_dim(pages, decode_prompt[group], 0, keepdims=False)

        outgoing = [pages_of(goes_to(me)) for goes_to, _ in partners(groups)]
        own = pages_of(me)
    blocks = [
        lax.ppermute(block, "group", [(i, goes_to(i)) for i in range(groups)])
        for block, (goes_to, _) in zip(outgoing, partners(groups))
    ]
    members = lax.axis_size(MEMBERS)

    def to_peer(array, distance):
        return lax.ppermute(array, MEMBERS, [(i, i ^ distance) for i in range(members)])

    packets = [to_peer(packet, at) for packet, at in zip(packets, PEERS)] + [packets[-1]]
    blocks = blocks + [own]
    sibling_blocks = [to_peer(block, SIBLING) for block in blocks]
    parts = attend(
        groups, steps, alive, arrange(steps, packets), blocks, sibling_blocks
    )
    cache = store(
        groups,
        page_table,
        [block.reshape(rows // PAGE, PAGE, 2 * HEAD_DIM) for block in blocks],
    )
    returned = gather([to_peer(part, at) for part, at in zip(parts, PEERS)] + [parts[-1]])
    attention_out = returned.reshape(KV_HEADS * Q_PER_KV, steps, HEAD_DIM).transpose(1, 0, 2)
    return attention_out.reshape(new_query.shape), cache[None]


def solution(mesh):
    return jax.shard_map(
        local,
        mesh=mesh,
        in_specs=(
            P(None, "group", None),
            P(None, MEMBERS),
            P(MEMBERS),
            P("group", MEMBERS, None, None),
            P("group", MEMBERS, None, None),
            P(),
            P(),
            P("group", None),
        ),
        out_specs=(P("group", MEMBERS, None, None), P("group", None, None, MEMBERS)),
        check_vma=False,
    )
```

```python
import functools
import math

import jax
import jax.numpy as jnp
from jax import lax
from jax.experimental import pallas as pl
from jax.experimental.pallas import tpu as pltpu
from jax.sharding import PartitionSpec as P

KV_HEADS = 8
HEAD_DIM = 128
Q_PER_KV = 8
PAGE = 8
ROPE_BASE = 1000000.0
MEMBERS = ("tp", "fork")
CHUNK = 1024
VMEM_LIMIT = 40 * 1024 * 1024
PACK_VMEM = 4 * 1024 * 1024
HIDE_FLOPS = 20 * 10**9


def partners(groups):
    if groups & (groups - 1) == 0:
        return [
            (lambda me, s=s: me ^ s, lambda me, s=s: me ^ s) for s in range(groups - 1, 0, -1)
        ]
    return [
        (lambda me, s=s: (me + s) % groups, lambda me, s=s: (me + groups - s) % groups)
        for s in range(1, groups)
    ]


SIBLING = 2
PEERS = (5, 4, 1)
NEAR, FAR = 1, 4
PACKETS = ((NEAR, NEAR ^ FAR), (FAR,), (0,))


def in_hbm(array):
    return pltpu.with_memory_space_constraint(array, pltpu.HBM)


def project_kernel(
    groups,
    ordered,
    prompt_hbm,
    count_hbm,
    x_hbm,
    w_hbm,
    b_hbm,
    query_hbm,
    recent_hbm,
    *rest,
):
    prompts = x_hbm.shape[0]
    outs, packed, rest = rest[:prompts], rest[prompts : prompts + 3], rest[prompts + 3 :]
    alive_ref, prompt_ref, count_ref, b_ref, query_ref, recent_ref, x_ref, w_ref, total_ref = rest[:9]
    small_sem, x_sem, w_sem = rest[9:]
    chunks, prompts, rows, depth = x_ref.shape
    small = [
        pltpu.make_async_copy(source, target, small_sem.at[at])
        for at, (source, target) in enumerate(
            [
                (prompt_hbm, prompt_ref),
                (count_hbm, count_ref),
                (b_hbm, b_ref),
                (recent_hbm, recent_ref),
                (query_hbm, query_ref),
            ]
        )
    ]

    def large(at):
        begin = pl.multiple_of(at * depth, depth)
        return (
            pltpu.make_async_copy(w_hbm.at[pl.ds(begin, depth)], w_ref.at[at], w_sem.at[at]),
            pltpu.make_async_copy(x_hbm.at[:, :, pl.ds(begin, depth)], x_ref.at[at], x_sem.at[at]),
        )

    for copy in small:
        copy.start()
    for at in range(chunks):
        for copy in large(at):
            copy.start()

    me = lax.axis_index("group")
    half = HEAD_DIM // 2
    lane = lax.broadcasted_iota(jnp.int32, (rows, HEAD_DIM), 1)
    index = jnp.where(lane < half, lane, lane - half).astype(jnp.float32)
    frequency = jnp.exp(index * (-2.0 * math.log(ROPE_BASE) / HEAD_DIM))
    position = me * rows + lax.broadcasted_iota(jnp.int32, (rows, HEAD_DIM), 0)
    angle = position.astype(jnp.float32) * frequency
    cosine = jnp.cos(angle)
    sine = jnp.sin(angle)
    sine = jnp.where(lane < half, -sine, sine)
    total_ref[...] = jnp.zeros_like(total_ref)

    def accumulate(at, carry):
        for copy in large(at):
            copy.wait()
        part = jnp.dot(
            x_ref[at].reshape(prompts * rows, depth),
            w_ref[at],
            preferred_element_type=jnp.float32,
        )
        total_ref[...] += part.reshape(total_ref.shape)
        return carry

    early = chunks - chunks // 4
    lax.fori_loop(0, early, accumulate, 0)
    for copy in small:
        copy.wait()
    q_rows = query_ref.shape[1]
    member = lax.axis_index(MEMBERS)
    for distances, packet in zip(PACKETS, packed):
        for to, distance in enumerate(distances):
            for at in range(2):
                head = member ^ distance ^ (SIBLING * at)
                packet[to, at, :q_rows, :] = query_ref[head]
                packet[to, at, q_rows:, :] = recent_ref[head]
    own_prompt = prompt_ref[me]
    earlier = jnp.int32(0)
    for g in range(groups):
        same = jnp.logical_and(g < me, prompt_ref[g] == own_prompt)
        earlier = earlier + jnp.where(same, 1, 0)
    limit = count_ref[own_prompt] - earlier * lax.axis_size(MEMBERS)
    for at, distance in enumerate(PEERS + (0,)):
        live = jnp.where((member ^ distance) < limit, 1.0, 0.0)
        alive_ref[at * q_rows : (at + 1) * q_rows, :] = jnp.full((q_rows, HEAD_DIM), live)
    lax.fori_loop(early, chunks, accumulate, 0)
    for at, out in enumerate(outs):
        prompt = at
        if ordered:
            prompt = prompt_ref[partners(groups)[at][0](me) if at < groups - 1 else me]
        total = total_ref[prompt] + b_ref[...]
        key = total[:, :HEAD_DIM]
        swapped = jnp.concatenate([key[:, half:], key[:, :half]], axis=1)
        out[:, :HEAD_DIM] = (key * cosine + swapped * sine).astype(out.dtype)
        out[:, HEAD_DIM:] = total[:, HEAD_DIM:].astype(out.dtype)


def project(groups, ordered, decode_prompt, sample_counts, prompt_hidden, kv_weight, kv_bias, query, recent):
    prompts, rows, depth = prompt_hidden.shape
    width = kv_weight.shape[1]
    chunks = depth // CHUNK
    packet_shape = (2, query.shape[1] + recent.shape[1], HEAD_DIM)
    packets = [pltpu.VMEM((len(to),) + packet_shape, query.dtype) for to in PACKETS]
    alive = pltpu.VMEM(((len(PEERS) + 1) * query.shape[1], HEAD_DIM), jnp.float32)
    bias = kv_bias.reshape(1, width)
    operands = (decode_prompt, sample_counts, prompt_hidden, kv_weight, bias, query, recent)
    return pl.pallas_call(
        functools.partial(project_kernel, groups, ordered),
        in_specs=[pl.BlockSpec(memory_space=pl.ANY)] * len(operands),
        out_specs=[pl.BlockSpec(memory_space=pltpu.VMEM)] * (prompts + len(packets) + 1),
        out_shape=[pltpu.VMEM((rows, width), jnp.bfloat16)] * prompts + packets + [alive],
        scratch_shapes=[
            pltpu.SMEM(decode_prompt.shape, jnp.int32),
            pltpu.SMEM(sample_counts.shape, jnp.int32),
            pltpu.VMEM((1, width), jnp.float32),
            pltpu.VMEM(query.shape, query.dtype),
            pltpu.VMEM(recent.shape, recent.dtype),
            pltpu.VMEM((chunks, prompts, rows, CHUNK), jnp.bfloat16),
            pltpu.VMEM((chunks, CHUNK, width), jnp.bfloat16),
            pltpu.VMEM((prompts, rows, width), jnp.float32),
            pltpu.SemaphoreType.DMA((5,)),
            pltpu.SemaphoreType.DMA((chunks,)),
            pltpu.SemaphoreType.DMA((chunks,)),
        ],
        compiler_params=pltpu.CompilerParams(vmem_limit_bytes=VMEM_LIMIT),
        name="project",
    )(*map(in_hbm, operands))


def store_kernel(groups, table_ref, *rest):
    blocks, (cache_ref, sem) = rest[:groups], rest[groups:]
    me = lax.axis_index("group")
    pages = blocks[0].shape[0]
    sources = [source(me) for _, source in partners(groups)] + [me]
    for block, source in zip(blocks, sources):

        def place(j, carry, block=block, source=source):
            slot = table_ref[0, source * pages + j]
            pltpu.make_async_copy(block.at[j], cache_ref.at[slot], sem).start()
            return carry

        lax.fori_loop(0, pages, place, 0, unroll=True)
    pltpu.make_async_copy(cache_ref, cache_ref, sem).wait()


def store(groups, page_table, blocks):
    return pl.pallas_call(
        functools.partial(store_kernel, groups),
        in_specs=[pl.BlockSpec(memory_space=pltpu.SMEM)]
        + [pl.BlockSpec(memory_space=pltpu.VMEM)] * groups,
        out_specs=pl.BlockSpec(memory_space=pl.ANY),
        out_shape=jax.ShapeDtypeStruct((page_table.shape[1],) + blocks[0].shape[1:], jnp.bfloat16),
        scratch_shapes=[pltpu.SemaphoreType.DMA],
        cost_estimate=pl.CostEstimate(flops=HIDE_FLOPS, transcendentals=0, bytes_accessed=0),
        compiler_params=pltpu.CompilerParams(vmem_limit_bytes=PACK_VMEM),
        name="store",
    )(page_table, *blocks)


def join_kernel(first_ref, second_ref, out_ref):
    out_ref[0] = first_ref[0]
    out_ref[1] = second_ref[1]


def join(first, second):
    vmem = pl.BlockSpec(memory_space=pltpu.VMEM)
    return pl.pallas_call(
        join_kernel,
        in_specs=[vmem] * 2,
        out_specs=vmem,
        out_shape=pltpu.VMEM(second.shape, second.dtype),
        compiler_params=pltpu.CompilerParams(vmem_limit_bytes=PACK_VMEM),
        name="join",
    )(first, second)


def arrange_kernel(steps, far_ref, near_ref, own_ref, query_ref, key_ref, value_ref):
    packets = (far_ref.at[1], far_ref.at[0], near_ref.at[0], own_ref.at[0])
    q_rows = Q_PER_KV * steps
    for at in range(2):
        recent = jnp.concatenate(
            [packet[at, q_rows:, :].astype(jnp.float32) for packet in packets], axis=0
        )
        shifted = jnp.concatenate([recent[steps:], recent[:steps]], axis=0)
        key_ref[at] = recent.astype(key_ref.dtype)
        value_ref[at] = shifted.astype(value_ref.dtype)
        for sample, packet in enumerate(packets):
            query_ref[at, sample * q_rows : (sample + 1) * q_rows, :] = packet[at, :q_rows, :]


def arrange(steps, packets):
    samples, dtype = len(PEERS) + 1, packets[0].dtype
    vmem = pl.BlockSpec(memory_space=pltpu.VMEM)
    recent = pltpu.VMEM((2, samples * 2 * steps, HEAD_DIM), dtype)
    return pl.pallas_call(
        functools.partial(arrange_kernel, steps),
        in_specs=[vmem] * 3,
        out_specs=[vmem] * 3,
        out_shape=[
            pltpu.VMEM((2, samples * Q_PER_KV * steps, HEAD_DIM), dtype),
            recent,
            recent,
        ],
        cost_estimate=pl.CostEstimate(flops=HIDE_FLOPS, transcendentals=0, bytes_accessed=0),
        compiler_params=pltpu.CompilerParams(vmem_limit_bytes=PACK_VMEM),
        name="arrange",
    )(*packets)


def attend_head(steps, alive, query, recent_key, recent_value, blocks):
    q_rows = Q_PER_KV * steps
    scaling = HEAD_DIM ** (-0.5)
    contract = (((1,), (1,)), ((), ()))

    def scored(keys):
        return (
            lax.dot_general(query, keys, contract, preferred_element_type=jnp.float32) * scaling
        )

    recent_score = scored(recent_key)
    row = lax.broadcasted_iota(jnp.int32, recent_score.shape, 0)
    column = lax.broadcasted_iota(jnp.int32, recent_score.shape, 1)
    visible = jnp.logical_and(
        row // q_rows == column // (2 * steps), column % (2 * steps) <= row % steps
    )
    recent_score = jnp.where(visible, recent_score, -jnp.inf)
    scores = [scored(block[:, :HEAD_DIM]) for block in blocks]
    highest = functools.reduce(jnp.maximum, scores).max(axis=1, keepdims=True)
    highest = jnp.maximum(highest, jnp.max(recent_score, axis=1, keepdims=True))
    recent_weight = jnp.exp(recent_score - highest)
    weights = [jnp.exp(score - highest) for score in scores]
    total = functools.reduce(jnp.add, weights).sum(axis=1, keepdims=True)
    total = total + jnp.sum(recent_weight, axis=1, keepdims=True)
    blended = jnp.dot(
        recent_weight.astype(jnp.bfloat16), recent_value, preferred_element_type=jnp.float32
    )
    for weight, block in zip(weights, blocks):
        blended = blended + jnp.dot(
            weight.astype(jnp.bfloat16), block[:, HEAD_DIM:], preferred_element_type=jnp.float32
        )
    blended = blended / total
    return jnp.where(alive > 0.0, blended, 0.0)


def attend_kernel(groups, steps, alive_ref, *rest):
    arranged, rest = rest[:3], rest[3:]
    head_blocks, outs = (rest[:groups], rest[groups : 2 * groups]), rest[2 * groups :]
    q_rows = Q_PER_KV * steps
    for at, refs in enumerate(head_blocks):
        blended = attend_head(
            steps,
            alive_ref[...],
            *[ref[at] for ref in arranged],
            [block[...] for block in refs],
        ).astype(jnp.bfloat16)
        for to, out in enumerate(outs):
            out[at] = blended[to * q_rows : (to + 1) * q_rows]


def attend(groups, steps, alive, arranged, own_blocks, sibling_blocks):
    packets = len(PEERS) + 1
    vmem = pl.BlockSpec(memory_space=pltpu.VMEM)
    return pl.pallas_call(
        functools.partial(attend_kernel, groups, steps),
        in_specs=[vmem] * (1 + len(arranged) + 2 * groups),
        out_specs=[vmem] * packets,
        out_shape=[pltpu.VMEM((2, Q_PER_KV * steps, HEAD_DIM), jnp.bfloat16)] * packets,
        compiler_params=pltpu.CompilerParams(vmem_limit_bytes=VMEM_LIMIT),
        name="attend",
    )(alive, *arranged, *own_blocks, *sibling_blocks)


def gather_kernel(*refs):
    parts, out_ref, sem = refs[:-2], refs[-2], refs[-1]
    member = lax.axis_index(MEMBERS)
    copies = []
    for distance, part in zip(PEERS + (0,), parts):
        for at in range(2):
            head = member ^ distance ^ (SIBLING * at)
            copies.append(
                pltpu.make_async_copy(part.at[at], out_ref.at[head], sem.at[len(copies)])
            )
    for copy in copies:
        copy.start()
    for copy in copies:
        copy.wait()


def gather(parts):
    heads, rows, width = 2 * len(parts), parts[0].shape[1], parts[0].shape[2]
    return pl.pallas_call(
        gather_kernel,
        in_specs=[pl.BlockSpec(memory_space=pltpu.VMEM)] * len(parts),
        out_specs=pl.BlockSpec(memory_space=pl.ANY),
        out_shape=pltpu.HBM((heads, rows, width), parts[0].dtype),
        scratch_shapes=[pltpu.SemaphoreType.DMA((heads,))],
        compiler_params=pltpu.CompilerParams(vmem_limit_bytes=PACK_VMEM),
        name="gather",
    )(*parts)


def local(
    prompt_hidden, kv_weight, kv_bias, new_query, new_kv, decode_prompt, sample_counts, page_table
):
    prompts, rows, _ = prompt_hidden.shape
    groups = lax.axis_size("group")
    steps = new_query.shape[2]
    me = lax.axis_index("group")
    ordered = groups == prompts

    by_head = new_query.reshape(steps, KV_HEADS, Q_PER_KV, HEAD_DIM).transpose(1, 2, 0, 3)
    kv_by_head = new_kv.reshape(steps, KV_HEADS, 2, HEAD_DIM).transpose(1, 2, 0, 3)
    results = project(
        groups,
        ordered,
        decode_prompt,
        sample_counts,
        prompt_hidden,
        kv_weight,
        kv_bias,
        by_head.reshape(KV_HEADS, Q_PER_KV * steps, HEAD_DIM),
        kv_by_head.reshape(KV_HEADS, 2 * steps, HEAD_DIM),
    )
    projected, packets, alive = results[:prompts], results[prompts:-1], results[-1]
    if ordered:
        outgoing, own = projected[:-1], projected[-1]
    else:
        pages = jnp.stack(projected)

        def pages_of(group):
            return lax.dynamic_index_in_dim(pages, decode_prompt[group], 0, keepdims=False)

        outgoing = [pages_of(goes_to(me)) for goes_to, _ in partners(groups)]
        own = pages_of(me)
    blocks = [
        lax.ppermute(block, "group", [(i, goes_to(i)) for i in range(groups)])
        for block, (goes_to, _) in zip(outgoing, partners(groups))
    ]
    members = lax.axis_size(MEMBERS)

    def to_peer(array, distance):
        return lax.ppermute(array, MEMBERS, [(i, i ^ distance) for i in range(members)])

    near, far, mine = packets
    near = to_peer(near, NEAR)
    packets = [to_peer(join(far, near), FAR), near, mine]
    blocks = blocks + [own]
    sibling_blocks = [to_peer(block, SIBLING) for block in blocks]
    parts = attend(
        groups, steps, alive, arrange(steps, packets), blocks, sibling_blocks
    )
    cache = store(
        groups,
        page_table,
        [block.reshape(rows // PAGE, PAGE, 2 * HEAD_DIM) for block in blocks],
    )
    returned = gather([to_peer(part, at) for part, at in zip(parts, PEERS)] + [parts[-1]])
    attention_out = returned.reshape(KV_HEADS * Q_PER_KV, steps, HEAD_DIM).transpose(1, 0, 2)
    return attention_out.reshape(new_query.shape), cache[None]


def solution(mesh):
    return jax.shard_map(
        local,
        mesh=mesh,
        in_specs=(
            P(None, "group", None),
            P(None, MEMBERS),
            P(MEMBERS),
            P("group", MEMBERS, None, None),
            P("group", MEMBERS, None, None),
            P(),
            P(),
            P("group", None),
        ),
        out_specs=(P("group", MEMBERS, None, None), P("group", None, None, MEMBERS)),
        check_vma=False,
    )
```

```python
import functools
import math

import jax
import jax.numpy as jnp
from jax import lax
from jax.experimental import pallas as pl
from jax.experimental.pallas import tpu as pltpu
from jax.sharding import PartitionSpec as P

KV_HEADS = 8
HEAD_DIM = 128
Q_PER_KV = 8
PAGE = 8
ROPE_BASE = 1000000.0
MEMBERS = ("tp", "fork")
CHUNK = 1024
VMEM_LIMIT = 40 * 1024 * 1024
PACK_VMEM = 4 * 1024 * 1024
HIDE_FLOPS = 20 * 10**9


def partners(groups):
    if groups & (groups - 1) == 0:
        return [
            (lambda me, s=s: me ^ s, lambda me, s=s: me ^ s) for s in range(groups - 1, 0, -1)
        ]
    return [
        (lambda me, s=s: (me + s) % groups, lambda me, s=s: (me + groups - s) % groups)
        for s in range(1, groups)
    ]


SIBLING = 2
PEERS = (5, 4, 1)
NEAR, FAR = 1, 4
PACKETS = ((NEAR, NEAR ^ FAR), (FAR,), (0,))


def in_hbm(array):
    return pltpu.with_memory_space_constraint(array, pltpu.HBM)


def project_kernel(
    groups,
    ordered,
    prompt_hbm,
    count_hbm,
    x_hbm,
    w_hbm,
    b_hbm,
    query_hbm,
    recent_hbm,
    *rest,
):
    prompts = x_hbm.shape[0]
    outs, packed, rest = rest[:prompts], rest[prompts : prompts + 3], rest[prompts + 3 :]
    alive_ref, prompt_ref, count_ref, b_ref, query_ref, recent_ref, x_ref, w_ref, total_ref = rest[:9]
    small_sem, x_sem, w_sem = rest[9:]
    chunks, prompts, rows, depth = x_ref.shape
    small = [
        pltpu.make_async_copy(source, target, small_sem.at[at])
        for at, (source, target) in enumerate(
            [
                (prompt_hbm, prompt_ref),
                (count_hbm, count_ref),
                (b_hbm, b_ref),
                (recent_hbm, recent_ref),
                (query_hbm, query_ref),
            ]
        )
    ]

    def large(at):
        begin = pl.multiple_of(at * depth, depth)
        return (
            pltpu.make_async_copy(w_hbm.at[pl.ds(begin, depth)], w_ref.at[at], w_sem.at[at]),
            pltpu.make_async_copy(x_hbm.at[:, :, pl.ds(begin, depth)], x_ref.at[at], x_sem.at[at]),
        )

    for copy in small:
        copy.start()
    for at in range(chunks):
        for copy in large(at):
            copy.start()

    me = lax.axis_index("group")
    half = HEAD_DIM // 2
    lane = lax.broadcasted_iota(jnp.int32, (rows, HEAD_DIM), 1)
    index = jnp.where(lane < half, lane, lane - half).astype(jnp.float32)
    frequency = jnp.exp(index * (-2.0 * math.log(ROPE_BASE) / HEAD_DIM))
    position = me * rows + lax.broadcasted_iota(jnp.int32, (rows, HEAD_DIM), 0)
    angle = position.astype(jnp.float32) * frequency
    cosine = jnp.cos(angle)
    sine = jnp.sin(angle)
    sine = jnp.where(lane < half, -sine, sine)
    total_ref[...] = jnp.zeros_like(total_ref)

    def accumulate(at, carry):
        for copy in large(at):
            copy.wait()
        part = jnp.dot(
            x_ref[at].reshape(prompts * rows, depth),
            w_ref[at],
            preferred_element_type=jnp.float32,
        )
        total_ref[...] += part.reshape(total_ref.shape)
        return carry

    early = chunks - chunks // 4
    lax.fori_loop(0, early, accumulate, 0)
    for copy in small:
        copy.wait()
    q_rows = query_ref.shape[1]
    member = lax.axis_index(MEMBERS)
    for distances, packet in zip(PACKETS, packed):
        for to, distance in enumerate(distances):
            for at in range(2):
                head = member ^ distance ^ (SIBLING * at)
                packet[to, at, :q_rows, :] = query_ref[head]
                packet[to, at, q_rows:, :] = recent_ref[head]
    own_prompt = prompt_ref[me]
    earlier = jnp.int32(0)
    for g in range(groups):
        same = jnp.logical_and(g < me, prompt_ref[g] == own_prompt)
        earlier = earlier + jnp.where(same, 1, 0)
    limit = count_ref[own_prompt] - earlier * lax.axis_size(MEMBERS)
    for at, distance in enumerate(PEERS + (0,)):
        live = jnp.where((member ^ distance) < limit, 1.0, 0.0)
        alive_ref[at * q_rows : (at + 1) * q_rows, :] = jnp.full((q_rows, HEAD_DIM), live)
    lax.fori_loop(early, chunks, accumulate, 0)
    for at, out in enumerate(outs):
        prompt = at
        if ordered:
            prompt = prompt_ref[partners(groups)[at][0](me) if at < groups - 1 else me]
        total = total_ref[prompt] + b_ref[...]
        key = total[:, :HEAD_DIM]
        swapped = jnp.concatenate([key[:, half:], key[:, :half]], axis=1)
        out[:, :HEAD_DIM] = (key * cosine + swapped * sine).astype(out.dtype)
        out[:, HEAD_DIM:] = total[:, HEAD_DIM:].astype(out.dtype)


def project(groups, ordered, decode_prompt, sample_counts, prompt_hidden, kv_weight, kv_bias, query, recent):
    prompts, rows, depth = prompt_hidden.shape
    width = kv_weight.shape[1]
    chunks = depth // CHUNK
    packet_shape = (2, query.shape[1] + recent.shape[1], HEAD_DIM)
    packets = [pltpu.VMEM((len(to),) + packet_shape, query.dtype) for to in PACKETS]
    alive = pltpu.VMEM(((len(PEERS) + 1) * query.shape[1], HEAD_DIM), jnp.float32)
    bias = kv_bias.reshape(1, width)
    operands = (decode_prompt, sample_counts, prompt_hidden, kv_weight, bias, query, recent)
    return pl.pallas_call(
        functools.partial(project_kernel, groups, ordered),
        in_specs=[pl.BlockSpec(memory_space=pl.ANY)] * len(operands),
        out_specs=[pl.BlockSpec(memory_space=pltpu.VMEM)] * (prompts + len(packets) + 1),
        out_shape=[pltpu.VMEM((rows, width), jnp.bfloat16)] * prompts + packets + [alive],
        scratch_shapes=[
            pltpu.SMEM(decode_prompt.shape, jnp.int32),
            pltpu.SMEM(sample_counts.shape, jnp.int32),
            pltpu.VMEM((1, width), jnp.float32),
            pltpu.VMEM(query.shape, query.dtype),
            pltpu.VMEM(recent.shape, recent.dtype),
            pltpu.VMEM((chunks, prompts, rows, CHUNK), jnp.bfloat16),
            pltpu.VMEM((chunks, CHUNK, width), jnp.bfloat16),
            pltpu.VMEM((prompts, rows, width), jnp.float32),
            pltpu.SemaphoreType.DMA((5,)),
            pltpu.SemaphoreType.DMA((chunks,)),
            pltpu.SemaphoreType.DMA((chunks,)),
        ],
        compiler_params=pltpu.CompilerParams(vmem_limit_bytes=VMEM_LIMIT),
        name="project",
    )(*map(in_hbm, operands))


def store_kernel(groups, table_ref, *rest):
    blocks, (cache_ref, sem) = rest[:groups], rest[groups:]
    me = lax.axis_index("group")
    pages = blocks[0].shape[0]
    sources = [source(me) for _, source in partners(groups)] + [me]
    for block, source in zip(blocks, sources):

        def place(j, carry, block=block, source=source):
            slot = table_ref[0, source * pages + j]
            pltpu.make_async_copy(block.at[j], cache_ref.at[slot], sem).start()
            return carry

        lax.fori_loop(0, pages, place, 0, unroll=True)
    pltpu.make_async_copy(cache_ref, cache_ref, sem).wait()


def store(groups, page_table, blocks):
    return pl.pallas_call(
        functools.partial(store_kernel, groups),
        in_specs=[pl.BlockSpec(memory_space=pltpu.SMEM)]
        + [pl.BlockSpec(memory_space=pltpu.VMEM)] * groups,
        out_specs=pl.BlockSpec(memory_space=pl.ANY),
        out_shape=jax.ShapeDtypeStruct((page_table.shape[1],) + blocks[0].shape[1:], jnp.bfloat16),
        scratch_shapes=[pltpu.SemaphoreType.DMA],
        cost_estimate=pl.CostEstimate(flops=HIDE_FLOPS, transcendentals=0, bytes_accessed=0),
        compiler_params=pltpu.CompilerParams(vmem_limit_bytes=PACK_VMEM),
        name="store",
    )(page_table, *blocks)


def join_kernel(first_ref, second_ref, out_ref):
    out_ref[0] = first_ref[0]
    out_ref[1] = second_ref[1]


def join(first, second):
    vmem = pl.BlockSpec(memory_space=pltpu.VMEM)
    return pl.pallas_call(
        join_kernel,
        in_specs=[vmem] * 2,
        out_specs=vmem,
        out_shape=pltpu.VMEM(second.shape, second.dtype),
        compiler_params=pltpu.CompilerParams(vmem_limit_bytes=PACK_VMEM),
        name="join",
    )(first, second)


def arrange_kernel(steps, far_ref, near_ref, own_ref, query_ref, key_ref, value_ref):
    packets = (far_ref.at[1], far_ref.at[0], near_ref.at[0], own_ref.at[0])
    q_rows = Q_PER_KV * steps
    for at in range(2):
        recent = jnp.concatenate(
            [packet[at, q_rows:, :].astype(jnp.float32) for packet in packets], axis=0
        )
        shifted = jnp.concatenate([recent[steps:], recent[:steps]], axis=0)
        key_ref[at] = recent.astype(key_ref.dtype)
        value_ref[at] = shifted.astype(value_ref.dtype)
        for sample, packet in enumerate(packets):
            query_ref[at, sample * q_rows : (sample + 1) * q_rows, :] = packet[at, :q_rows, :]


def arrange(steps, packets):
    samples, dtype = len(PEERS) + 1, packets[0].dtype
    vmem = pl.BlockSpec(memory_space=pltpu.VMEM)
    recent = pltpu.VMEM((2, samples * 2 * steps, HEAD_DIM), dtype)
    return pl.pallas_call(
        functools.partial(arrange_kernel, steps),
        in_specs=[vmem] * 3,
        out_specs=[vmem] * 3,
        out_shape=[
            pltpu.VMEM((2, samples * Q_PER_KV * steps, HEAD_DIM), dtype),
            recent,
            recent,
        ],
        cost_estimate=pl.CostEstimate(flops=HIDE_FLOPS, transcendentals=0, bytes_accessed=0),
        compiler_params=pltpu.CompilerParams(vmem_limit_bytes=PACK_VMEM),
        name="arrange",
    )(*packets)


def attend_head(steps, alive, query, recent_key, recent_value, blocks):
    q_rows = Q_PER_KV * steps
    scaling = HEAD_DIM ** (-0.5)
    contract = (((1,), (1,)), ((), ()))

    def scored(keys):
        return (
            lax.dot_general(query, keys, contract, preferred_element_type=jnp.float32) * scaling
        )

    recent_score = scored(recent_key)
    row = lax.broadcasted_iota(jnp.int32, recent_score.shape, 0)
    column = lax.broadcasted_iota(jnp.int32, recent_score.shape, 1)
    visible = jnp.logical_and(
        row // q_rows == column // (2 * steps), column % (2 * steps) <= row % steps
    )
    recent_score = jnp.where(visible, recent_score, -jnp.inf)
    scores = [scored(block[:, :HEAD_DIM]) for block in blocks]
    highest = functools.reduce(jnp.maximum, scores).max(axis=1, keepdims=True)
    highest = jnp.maximum(highest, jnp.max(recent_score, axis=1, keepdims=True))
    recent_weight = jnp.exp(recent_score - highest)
    weights = [jnp.exp(score - highest) for score in scores]
    total = functools.reduce(jnp.add, weights).sum(axis=1, keepdims=True)
    total = total + jnp.sum(recent_weight, axis=1, keepdims=True)
    blended = jnp.dot(
        recent_weight.astype(jnp.bfloat16), recent_value, preferred_element_type=jnp.float32
    )
    for weight, block in zip(weights, blocks):
        blended = blended + jnp.dot(
            weight.astype(jnp.bfloat16), block[:, HEAD_DIM:], preferred_element_type=jnp.float32
        )
    blended = blended / total
    return jnp.where(alive > 0.0, blended, 0.0)


def attend_own_kernel(groups, steps, alive_ref, query_ref, key_ref, value_ref, *rest):
    blocks, out_ref = rest[:groups], rest[groups]
    out_ref[...] = attend_head(
        steps,
        alive_ref[...],
        query_ref[0],
        key_ref[0],
        value_ref[0],
        [block[...] for block in blocks],
    ).astype(out_ref.dtype)


def attend_own(groups, steps, alive, arranged, blocks):
    vmem = pl.BlockSpec(memory_space=pltpu.VMEM)
    return pl.pallas_call(
        functools.partial(attend_own_kernel, groups, steps),
        in_specs=[vmem] * (1 + len(arranged) + groups),
        out_specs=vmem,
        out_shape=pltpu.VMEM(arranged[0].shape[1:], jnp.bfloat16),
        cost_estimate=pl.CostEstimate(flops=HIDE_FLOPS, transcendentals=0, bytes_accessed=0),
        compiler_params=pltpu.CompilerParams(vmem_limit_bytes=VMEM_LIMIT),
        name="attend_own",
    )(alive, *arranged, *blocks)


def attend_kernel(groups, steps, alive_ref, query_ref, key_ref, value_ref, own_ref, *rest):
    blocks, outs = rest[:groups], rest[groups:]
    q_rows = Q_PER_KV * steps
    blended = attend_head(
        steps,
        alive_ref[...],
        query_ref[1],
        key_ref[1],
        value_ref[1],
        [block[...] for block in blocks],
    ).astype(jnp.bfloat16)
    for to, out in enumerate(outs):
        out[0] = own_ref[to * q_rows : (to + 1) * q_rows]
        out[1] = blended[to * q_rows : (to + 1) * q_rows]


def attend(groups, steps, alive, arranged, own, blocks):
    packets = len(PEERS) + 1
    vmem = pl.BlockSpec(memory_space=pltpu.VMEM)
    return pl.pallas_call(
        functools.partial(attend_kernel, groups, steps),
        in_specs=[vmem] * (2 + len(arranged) + groups),
        out_specs=[vmem] * packets,
        out_shape=[pltpu.VMEM((2, Q_PER_KV * steps, HEAD_DIM), jnp.bfloat16)] * packets,
        compiler_params=pltpu.CompilerParams(vmem_limit_bytes=VMEM_LIMIT),
        name="attend",
    )(alive, *arranged, own, *blocks)


def gather_kernel(*refs):
    parts, out_ref, sem = refs[:-2], refs[-2], refs[-1]
    member = lax.axis_index(MEMBERS)
    copies = []
    for distance, part in zip(PEERS + (0,), parts):
        for at in range(2):
            head = member ^ distance ^ (SIBLING * at)
            copies.append(
                pltpu.make_async_copy(part.at[at], out_ref.at[head], sem.at[len(copies)])
            )
    for copy in copies:
        copy.start()
    for copy in copies:
        copy.wait()


def gather(parts):
    heads, rows, width = 2 * len(parts), parts[0].shape[1], parts[0].shape[2]
    return pl.pallas_call(
        gather_kernel,
        in_specs=[pl.BlockSpec(memory_space=pltpu.VMEM)] * len(parts),
        out_specs=pl.BlockSpec(memory_space=pl.ANY),
        out_shape=pltpu.HBM((heads, rows, width), parts[0].dtype),
        scratch_shapes=[pltpu.SemaphoreType.DMA((heads,))],
        compiler_params=pltpu.CompilerParams(vmem_limit_bytes=PACK_VMEM),
        name="gather",
    )(*parts)


def local(
    prompt_hidden, kv_weight, kv_bias, new_query, new_kv, decode_prompt, sample_counts, page_table
):
    prompts, rows, _ = prompt_hidden.shape
    groups = lax.axis_size("group")
    steps = new_query.shape[2]
    me = lax.axis_index("group")
    ordered = groups == prompts

    by_head = new_query.reshape(steps, KV_HEADS, Q_PER_KV, HEAD_DIM).transpose(1, 2, 0, 3)
    kv_by_head = new_kv.reshape(steps, KV_HEADS, 2, HEAD_DIM).transpose(1, 2, 0, 3)
    results = project(
        groups,
        ordered,
        decode_prompt,
        sample_counts,
        prompt_hidden,
        kv_weight,
        kv_bias,
        by_head.reshape(KV_HEADS, Q_PER_KV * steps, HEAD_DIM),
        kv_by_head.reshape(KV_HEADS, 2 * steps, HEAD_DIM),
    )
    projected, packets, alive = results[:prompts], results[prompts:-1], results[-1]
    if ordered:
        outgoing, own = projected[:-1], projected[-1]
    else:
        pages = jnp.stack(projected)

        def pages_of(group):
            return lax.dynamic_index_in_dim(pages, decode_prompt[group], 0, keepdims=False)

        outgoing = [pages_of(goes_to(me)) for goes_to, _ in partners(groups)]
        own = pages_of(me)
    blocks = [
        lax.ppermute(block, "group", [(i, goes_to(i)) for i in range(groups)])
        for block, (goes_to, _) in zip(outgoing, partners(groups))
    ]
    members = lax.axis_size(MEMBERS)

    def to_peer(array, distance):
        return lax.ppermute(array, MEMBERS, [(i, i ^ distance) for i in range(members)])

    near, far, mine = packets
    near = to_peer(near, NEAR)
    packets = [to_peer(join(far, near), FAR), near, mine]
    blocks = blocks + [own]
    ready = [own] + blocks[:-3] + [blocks[-2], blocks[-3]]
    sibling_blocks = [to_peer(block, SIBLING) for block in ready]
    arranged = arrange(steps, packets)
    own_head = attend_own(groups, steps, alive, arranged, ready)
    parts = attend(groups, steps, alive, arranged, own_head, sibling_blocks)
    cache = store(
        groups,
        page_table,
        [block.reshape(rows // PAGE, PAGE, 2 * HEAD_DIM) for block in blocks],
    )
    returned = gather([to_peer(part, at) for part, at in zip(parts, PEERS)] + [parts[-1]])
    attention_out = returned.reshape(KV_HEADS * Q_PER_KV, steps, HEAD_DIM).transpose(1, 0, 2)
    return attention_out.reshape(new_query.shape), cache[None]


def solution(mesh):
    return jax.shard_map(
        local,
        mesh=mesh,
        in_specs=(
            P(None, "group", None),
            P(None, MEMBERS),
            P(MEMBERS),
            P("group", MEMBERS, None, None),
            P("group", MEMBERS, None, None),
            P(),
            P(),
            P("group", None),
        ),
        out_specs=(P("group", MEMBERS, None, None), P("group", None, None, MEMBERS)),
        check_vma=False,
    )
```

```python
import functools
import math

import jax
import jax.numpy as jnp
from jax import lax
from jax.experimental import pallas as pl
from jax.experimental.pallas import tpu as pltpu
from jax.sharding import PartitionSpec as P

KV_HEADS = 8
HEAD_DIM = 128
Q_PER_KV = 8
PAGE = 8
ROPE_BASE = 1000000.0
MEMBERS = ("tp", "fork")
CHUNK = 1024
VMEM_LIMIT = 40 * 1024 * 1024
PACK_VMEM = 4 * 1024 * 1024
HIDE_FLOPS = 20 * 10**9


def partners(groups):
    if groups & (groups - 1) == 0:
        return [
            (lambda me, s=s: me ^ s, lambda me, s=s: me ^ s) for s in range(groups - 1, 0, -1)
        ]
    return [
        (lambda me, s=s: (me + s) % groups, lambda me, s=s: (me + groups - s) % groups)
        for s in range(1, groups)
    ]


SIBLING = 2
PEERS = (5, 4, 1)
NEAR, FAR = 1, 4
PACKETS = ((NEAR, NEAR ^ FAR), (FAR,), (0,))


def in_hbm(array):
    return pltpu.with_memory_space_constraint(array, pltpu.HBM)


def project_kernel(
    groups,
    ordered,
    prompt_hbm,
    count_hbm,
    x_hbm,
    w_hbm,
    b_hbm,
    query_hbm,
    recent_hbm,
    *rest,
):
    prompts = x_hbm.shape[0]
    outs, packed, rest = rest[:prompts], rest[prompts : prompts + 3], rest[prompts + 3 :]
    alive_ref, prompt_ref, count_ref, b_ref, query_ref, recent_ref, x_ref, w_ref, total_ref = rest[:9]
    small_sem, x_sem, w_sem = rest[9:]
    chunks, prompts, rows, depth = x_ref.shape
    small = [
        pltpu.make_async_copy(source, target, small_sem.at[at])
        for at, (source, target) in enumerate(
            [
                (prompt_hbm, prompt_ref),
                (count_hbm, count_ref),
                (b_hbm, b_ref),
                (recent_hbm, recent_ref),
                (query_hbm, query_ref),
            ]
        )
    ]

    def large(at):
        begin = pl.multiple_of(at * depth, depth)
        return (
            pltpu.make_async_copy(w_hbm.at[pl.ds(begin, depth)], w_ref.at[at], w_sem.at[at]),
            pltpu.make_async_copy(x_hbm.at[:, :, pl.ds(begin, depth)], x_ref.at[at], x_sem.at[at]),
        )

    for copy in small:
        copy.start()
    for at in range(chunks):
        for copy in large(at):
            copy.start()

    me = lax.axis_index("group")
    half = HEAD_DIM // 2
    lane = lax.broadcasted_iota(jnp.int32, (rows, HEAD_DIM), 1)
    index = jnp.where(lane < half, lane, lane - half).astype(jnp.float32)
    frequency = jnp.exp(index * (-2.0 * math.log(ROPE_BASE) / HEAD_DIM))
    position = me * rows + lax.broadcasted_iota(jnp.int32, (rows, HEAD_DIM), 0)
    angle = position.astype(jnp.float32) * frequency
    cosine = jnp.cos(angle)
    sine = jnp.sin(angle)
    sine = jnp.where(lane < half, -sine, sine)
    total_ref[...] = jnp.zeros_like(total_ref)

    def accumulate(at, carry):
        for copy in large(at):
            copy.wait()
        part = jnp.dot(
            x_ref[at].reshape(prompts * rows, depth),
            w_ref[at],
            preferred_element_type=jnp.float32,
        )
        total_ref[...] += part.reshape(total_ref.shape)
        return carry

    early = chunks - chunks // 4
    lax.fori_loop(0, early, accumulate, 0)
    for copy in small:
        copy.wait()
    q_rows = query_ref.shape[1]
    member = lax.axis_index(MEMBERS)
    for distances, packet in zip(PACKETS, packed):
        for to, distance in enumerate(distances):
            for at in range(2):
                head = member ^ distance ^ (SIBLING * at)
                packet[to, at, :q_rows, :] = query_ref[head]
                packet[to, at, q_rows:, :] = recent_ref[head]
    own_prompt = prompt_ref[me]
    earlier = jnp.int32(0)
    for g in range(groups):
        same = jnp.logical_and(g < me, prompt_ref[g] == own_prompt)
        earlier = earlier + jnp.where(same, 1, 0)
    limit = count_ref[own_prompt] - earlier * lax.axis_size(MEMBERS)
    for at, distance in enumerate(PEERS + (0,)):
        live = jnp.where((member ^ distance) < limit, 1.0, 0.0)
        alive_ref[at * q_rows : (at + 1) * q_rows, :] = jnp.full((q_rows, HEAD_DIM), live)
    lax.fori_loop(early, chunks, accumulate, 0)
    for at, out in enumerate(outs):
        prompt = at
        if ordered:
            prompt = prompt_ref[partners(groups)[at][0](me) if at < groups - 1 else me]
        total = total_ref[prompt] + b_ref[...]
        key = total[:, :HEAD_DIM]
        swapped = jnp.concatenate([key[:, half:], key[:, :half]], axis=1)
        out[:, :HEAD_DIM] = (key * cosine + swapped * sine).astype(out.dtype)
        out[:, HEAD_DIM:] = total[:, HEAD_DIM:].astype(out.dtype)


def project(groups, ordered, decode_prompt, sample_counts, prompt_hidden, kv_weight, kv_bias, query, recent):
    prompts, rows, depth = prompt_hidden.shape
    width = kv_weight.shape[1]
    chunks = depth // CHUNK
    packet_shape = (2, query.shape[1] + recent.shape[1], HEAD_DIM)
    packets = [pltpu.VMEM((len(to),) + packet_shape, query.dtype) for to in PACKETS]
    alive = pltpu.VMEM(((len(PEERS) + 1) * query.shape[1], HEAD_DIM), jnp.float32)
    bias = kv_bias.reshape(1, width)
    operands = (decode_prompt, sample_counts, prompt_hidden, kv_weight, bias, query, recent)
    return pl.pallas_call(
        functools.partial(project_kernel, groups, ordered),
        in_specs=[pl.BlockSpec(memory_space=pl.ANY)] * len(operands),
        out_specs=[pl.BlockSpec(memory_space=pltpu.VMEM)] * (prompts + len(packets) + 1),
        out_shape=[pltpu.VMEM((rows, width), jnp.bfloat16)] * prompts + packets + [alive],
        scratch_shapes=[
            pltpu.SMEM(decode_prompt.shape, jnp.int32),
            pltpu.SMEM(sample_counts.shape, jnp.int32),
            pltpu.VMEM((1, width), jnp.float32),
            pltpu.VMEM(query.shape, query.dtype),
            pltpu.VMEM(recent.shape, recent.dtype),
            pltpu.VMEM((chunks, prompts, rows, CHUNK), jnp.bfloat16),
            pltpu.VMEM((chunks, CHUNK, width), jnp.bfloat16),
            pltpu.VMEM((prompts, rows, width), jnp.float32),
            pltpu.SemaphoreType.DMA((5,)),
            pltpu.SemaphoreType.DMA((chunks,)),
            pltpu.SemaphoreType.DMA((chunks,)),
        ],
        compiler_params=pltpu.CompilerParams(vmem_limit_bytes=VMEM_LIMIT),
        name="project",
    )(*map(in_hbm, operands))


def store_kernel(groups, picks, table_ref, *rest):
    blocks, (cache_ref, sem) = rest[: len(picks)], rest[-2:]
    me = lax.axis_index("group")
    pages = blocks[0].shape[0]
    sources = [source(me) for _, source in partners(groups)] + [me]
    for block, at in zip(blocks, picks):

        def place(j, carry, block=block, source=sources[at]):
            slot = table_ref[0, source * pages + j]
            pltpu.make_async_copy(block.at[j], cache_ref.at[slot], sem).start()
            return carry

        lax.fori_loop(0, pages, place, 0, unroll=True)
    stored = cache_ref.at[pl.ds(0, len(picks) * pages)]
    pltpu.make_async_copy(stored, stored, sem).wait()


def store(groups, picks, page_table, blocks, cache=None):
    pages = rows_of(blocks)
    operands = [page_table] + pages
    specs = [pl.BlockSpec(memory_space=pltpu.SMEM)] + [pl.BlockSpec(memory_space=pltpu.VMEM)] * len(pages)
    aliases = {}
    if cache is not None:
        aliases = {len(operands): 0}
        operands.append(cache)
        specs.append(pl.BlockSpec(memory_space=pl.ANY))
    return pl.pallas_call(
        functools.partial(store_kernel, groups, picks),
        in_specs=specs,
        out_specs=pl.BlockSpec(memory_space=pl.ANY),
        out_shape=pltpu.HBM((page_table.shape[1],) + pages[0].shape[1:], jnp.bfloat16),
        input_output_aliases=aliases,
        scratch_shapes=[pltpu.SemaphoreType.DMA],
        cost_estimate=pl.CostEstimate(flops=HIDE_FLOPS, transcendentals=0, bytes_accessed=0),
        compiler_params=pltpu.CompilerParams(vmem_limit_bytes=PACK_VMEM),
        name="store",
    )(*operands)


def rows_of(blocks):
    return [block.reshape(block.shape[0] // PAGE, PAGE, 2 * HEAD_DIM) for block in blocks]


def join_kernel(first_ref, second_ref, out_ref):
    out_ref[0] = first_ref[0]
    out_ref[1] = second_ref[1]


def join(first, second):
    vmem = pl.BlockSpec(memory_space=pltpu.VMEM)
    return pl.pallas_call(
        join_kernel,
        in_specs=[vmem] * 2,
        out_specs=vmem,
        out_shape=pltpu.VMEM(second.shape, second.dtype),
        compiler_params=pltpu.CompilerParams(vmem_limit_bytes=PACK_VMEM),
        name="join",
    )(first, second)


def arrange_kernel(steps, far_ref, near_ref, own_ref, query_ref, key_ref, value_ref):
    packets = (far_ref.at[1], far_ref.at[0], near_ref.at[0], own_ref.at[0])
    q_rows = Q_PER_KV * steps
    for at in range(2):
        recent = jnp.concatenate(
            [packet[at, q_rows:, :].astype(jnp.float32) for packet in packets], axis=0
        )
        shifted = jnp.concatenate([recent[steps:], recent[:steps]], axis=0)
        key_ref[at] = recent.astype(key_ref.dtype)
        value_ref[at] = shifted.astype(value_ref.dtype)
        for sample, packet in enumerate(packets):
            query_ref[at, sample * q_rows : (sample + 1) * q_rows, :] = packet[at, :q_rows, :]


def arrange(steps, packets):
    samples, dtype = len(PEERS) + 1, packets[0].dtype
    vmem = pl.BlockSpec(memory_space=pltpu.VMEM)
    recent = pltpu.VMEM((2, samples * 2 * steps, HEAD_DIM), dtype)
    return pl.pallas_call(
        functools.partial(arrange_kernel, steps),
        in_specs=[vmem] * 3,
        out_specs=[vmem] * 3,
        out_shape=[
            pltpu.VMEM((2, samples * Q_PER_KV * steps, HEAD_DIM), dtype),
            recent,
            recent,
        ],
        cost_estimate=pl.CostEstimate(flops=HIDE_FLOPS, transcendentals=0, bytes_accessed=0),
        compiler_params=pltpu.CompilerParams(vmem_limit_bytes=PACK_VMEM),
        name="arrange",
    )(*packets)


def attend_head(steps, alive, query, recent_key, recent_value, blocks):
    q_rows = Q_PER_KV * steps
    scaling = HEAD_DIM ** (-0.5)
    contract = (((1,), (1,)), ((), ()))

    def scored(keys):
        return (
            lax.dot_general(query, keys, contract, preferred_element_type=jnp.float32) * scaling
        )

    recent_score = scored(recent_key)
    row = lax.broadcasted_iota(jnp.int32, recent_score.shape, 0)
    column = lax.broadcasted_iota(jnp.int32, recent_score.shape, 1)
    visible = jnp.logical_and(
        row // q_rows == column // (2 * steps), column % (2 * steps) <= row % steps
    )
    recent_score = jnp.where(visible, recent_score, -jnp.inf)
    score = scored(jnp.concatenate([block[:, :HEAD_DIM] for block in blocks], axis=0))
    highest = jnp.max(score, axis=1, keepdims=True)
    highest = jnp.maximum(highest, jnp.max(recent_score, axis=1, keepdims=True))
    recent_weight = jnp.exp(recent_score - highest)
    weight = jnp.exp(score - highest)
    total = jnp.sum(weight, axis=1, keepdims=True)
    total = total + jnp.sum(recent_weight, axis=1, keepdims=True)
    values = jnp.concatenate([block[:, HEAD_DIM:] for block in blocks], axis=0)
    blended = jnp.dot(
        recent_weight.astype(jnp.bfloat16), recent_value, preferred_element_type=jnp.float32
    ) + jnp.dot(weight.astype(jnp.bfloat16), values, preferred_element_type=jnp.float32)
    blended = blended / total
    return jnp.where(alive > 0.0, blended, 0.0)


def attend_own_kernel(groups, steps, cache_ref, alive_ref, query_ref, key_ref, value_ref, *rest):
    del cache_ref
    blocks, out_ref = rest[:groups], rest[groups]
    out_ref[...] = attend_head(
        steps,
        alive_ref[...],
        query_ref[0],
        key_ref[0],
        value_ref[0],
        [block[...] for block in blocks],
    ).astype(out_ref.dtype)


def attend_own(groups, steps, cache, alive, arranged, blocks):
    vmem = pl.BlockSpec(memory_space=pltpu.VMEM)
    return pl.pallas_call(
        functools.partial(attend_own_kernel, groups, steps),
        in_specs=[pl.BlockSpec(memory_space=pl.ANY)] + [vmem] * (1 + len(arranged) + groups),
        out_specs=vmem,
        out_shape=pltpu.VMEM(arranged[0].shape[1:], jnp.bfloat16),
        cost_estimate=pl.CostEstimate(flops=HIDE_FLOPS, transcendentals=0, bytes_accessed=0),
        compiler_params=pltpu.CompilerParams(vmem_limit_bytes=VMEM_LIMIT),
        name="attend_own",
    )(in_hbm(cache), alive, *arranged, *blocks)


def attend_kernel(groups, steps, alive_ref, query_ref, key_ref, value_ref, own_ref, *rest):
    blocks, outs = rest[:groups], rest[groups:]
    q_rows = Q_PER_KV * steps
    blended = attend_head(
        steps,
        alive_ref[...],
        query_ref[1],
        key_ref[1],
        value_ref[1],
        [block[...] for block in blocks],
    ).astype(jnp.bfloat16)
    for to, out in enumerate(outs):
        out[0] = own_ref[to * q_rows : (to + 1) * q_rows]
        out[1] = blended[to * q_rows : (to + 1) * q_rows]


def attend(groups, steps, alive, arranged, own, blocks):
    packets = len(PEERS) + 1
    vmem = pl.BlockSpec(memory_space=pltpu.VMEM)
    return pl.pallas_call(
        functools.partial(attend_kernel, groups, steps),
        in_specs=[vmem] * (2 + len(arranged) + groups),
        out_specs=[vmem] * packets,
        out_shape=[pltpu.VMEM((2, Q_PER_KV * steps, HEAD_DIM), jnp.bfloat16)] * packets,
        compiler_params=pltpu.CompilerParams(vmem_limit_bytes=VMEM_LIMIT),
        name="attend",
    )(alive, *arranged, own, *blocks)


def gather_kernel(*refs):
    parts, out_ref, sem = refs[:-2], refs[-2], refs[-1]
    member = lax.axis_index(MEMBERS)
    copies = []
    for distance, part in zip(PEERS + (0,), parts):
        for at in range(2):
            head = member ^ distance ^ (SIBLING * at)
            copies.append(
                pltpu.make_async_copy(part.at[at], out_ref.at[head], sem.at[len(copies)])
            )
    for copy in copies:
        copy.start()
    for copy in copies:
        copy.wait()


def gather(parts):
    heads, rows, width = 2 * len(parts), parts[0].shape[1], parts[0].shape[2]
    return pl.pallas_call(
        gather_kernel,
        in_specs=[pl.BlockSpec(memory_space=pltpu.VMEM)] * len(parts),
        out_specs=pl.BlockSpec(memory_space=pl.ANY),
        out_shape=pltpu.HBM((heads, rows, width), parts[0].dtype),
        scratch_shapes=[pltpu.SemaphoreType.DMA((heads,))],
        compiler_params=pltpu.CompilerParams(vmem_limit_bytes=PACK_VMEM),
        name="gather",
    )(*parts)


def local(
    prompt_hidden, kv_weight, kv_bias, new_query, new_kv, decode_prompt, sample_counts, page_table
):
    prompts, rows, _ = prompt_hidden.shape
    groups = lax.axis_size("group")
    steps = new_query.shape[2]
    me = lax.axis_index("group")
    ordered = groups == prompts

    by_head = new_query.reshape(steps, KV_HEADS, Q_PER_KV, HEAD_DIM).transpose(1, 2, 0, 3)
    kv_by_head = new_kv.reshape(steps, KV_HEADS, 2, HEAD_DIM).transpose(1, 2, 0, 3)
    results = project(
        groups,
        ordered,
        decode_prompt,
        sample_counts,
        prompt_hidden,
        kv_weight,
        kv_bias,
        by_head.reshape(KV_HEADS, Q_PER_KV * steps, HEAD_DIM),
        kv_by_head.reshape(KV_HEADS, 2 * steps, HEAD_DIM),
    )
    projected, packets, alive = results[:prompts], results[prompts:-1], results[-1]
    if ordered:
        outgoing, own = projected[:-1], projected[-1]
    else:
        pages = jnp.stack(projected)

        def pages_of(group):
            return lax.dynamic_index_in_dim(pages, decode_prompt[group], 0, keepdims=False)

        outgoing = [pages_of(goes_to(me)) for goes_to, _ in partners(groups)]
        own = pages_of(me)
    blocks = [
        lax.ppermute(block, "group", [(i, goes_to(i)) for i in range(groups)])
        for block, (goes_to, _) in zip(outgoing, partners(groups))
    ]
    members = lax.axis_size(MEMBERS)

    def to_peer(array, distance):
        return lax.ppermute(array, MEMBERS, [(i, i ^ distance) for i in range(members)])

    near, far, mine = packets
    near = to_peer(near, NEAR)
    packets = [to_peer(join(far, near), FAR), near, mine]
    blocks = blocks + [own]
    ready = [own] + blocks[:-3] + [blocks[-2], blocks[-3]]
    sibling_blocks = [to_peer(block, SIBLING) for block in ready]
    arranged = arrange(steps, packets)
    early = (groups - 1,)
    cache = store(groups, early, page_table, [blocks[at] for at in early])
    own_head = attend_own(groups, steps, cache, alive, arranged, ready)
    parts = attend(groups, steps, alive, arranged, own_head, sibling_blocks)
    late = tuple(at for at in range(groups) if at not in early)
    cache = store(groups, late, page_table, [blocks[at] for at in late], cache)
    returned = gather([to_peer(part, at) for part, at in zip(parts, PEERS)] + [parts[-1]])
    attention_out = returned.reshape(KV_HEADS * Q_PER_KV, steps, HEAD_DIM).transpose(1, 0, 2)
    return attention_out.reshape(new_query.shape), cache[None]


def solution(mesh):
    return jax.shard_map(
        local,
        mesh=mesh,
        in_specs=(
            P(None, "group", None),
            P(None, MEMBERS),
            P(MEMBERS),
            P("group", MEMBERS, None, None),
            P("group", MEMBERS, None, None),
            P(),
            P(),
            P("group", None),
        ),
        out_specs=(P("group", MEMBERS, None, None), P("group", None, None, MEMBERS)),
        check_vma=False,
    )
```

```python
import functools
import math

import jax
import jax.numpy as jnp
from jax import lax
from jax.experimental import pallas as pl
from jax.experimental.pallas import tpu as pltpu
from jax.sharding import PartitionSpec as P

KV_HEADS = 8
HEAD_DIM = 128
Q_PER_KV = 8
PAGE = 8
ROPE_BASE = 1000000.0
MEMBERS = ("tp", "fork")
CHUNK = 1024
VMEM_LIMIT = 40 * 1024 * 1024
PACK_VMEM = 4 * 1024 * 1024
HIDE_FLOPS = 20 * 10**9


def partners(groups):
    if groups & (groups - 1) == 0:
        return [
            (lambda me, s=s: me ^ s, lambda me, s=s: me ^ s) for s in range(groups - 1, 0, -1)
        ]
    return [
        (lambda me, s=s: (me + s) % groups, lambda me, s=s: (me + groups - s) % groups)
        for s in range(1, groups)
    ]


SIBLING = 2
PEERS = (5, 4, 1)
NEAR, FAR = 1, 4
PACKETS = ((NEAR, NEAR ^ FAR), (FAR,), (0,))


def in_hbm(array):
    return pltpu.with_memory_space_constraint(array, pltpu.HBM)


def project_kernel(
    groups,
    ordered,
    prompt_hbm,
    count_hbm,
    x_hbm,
    w_hbm,
    b_hbm,
    query_hbm,
    recent_hbm,
    *rest,
):
    prompts = x_hbm.shape[0]
    outs, packed, rest = rest[:prompts], rest[prompts : prompts + 3], rest[prompts + 3 :]
    alive_ref, prompt_ref, count_ref, b_ref, query_ref, recent_ref, x_ref, w_ref, total_ref = rest[:9]
    small_sem, x_sem, w_sem = rest[9:]
    chunks, prompts, rows, depth = x_ref.shape
    small = [
        pltpu.make_async_copy(source, target, small_sem.at[at])
        for at, (source, target) in enumerate(
            [
                (prompt_hbm, prompt_ref),
                (count_hbm, count_ref),
                (b_hbm, b_ref),
                (recent_hbm, recent_ref),
                (query_hbm, query_ref),
            ]
        )
    ]

    def large(at):
        begin = pl.multiple_of(at * depth, depth)
        return (
            pltpu.make_async_copy(w_hbm.at[pl.ds(begin, depth)], w_ref.at[at], w_sem.at[at]),
            pltpu.make_async_copy(x_hbm.at[:, :, pl.ds(begin, depth)], x_ref.at[at], x_sem.at[at]),
        )

    for copy in small:
        copy.start()
    for at in range(chunks):
        for copy in large(at):
            copy.start()

    me = lax.axis_index("group")
    half = HEAD_DIM // 2
    lane = lax.broadcasted_iota(jnp.int32, (rows, HEAD_DIM), 1)
    index = jnp.where(lane < half, lane, lane - half).astype(jnp.float32)
    frequency = jnp.exp(index * (-2.0 * math.log(ROPE_BASE) / HEAD_DIM))
    position = me * rows + lax.broadcasted_iota(jnp.int32, (rows, HEAD_DIM), 0)
    angle = position.astype(jnp.float32) * frequency
    cosine = jnp.cos(angle)
    sine = jnp.sin(angle)
    sine = jnp.where(lane < half, -sine, sine)
    total_ref[...] = jnp.zeros_like(total_ref)

    def accumulate(at, carry):
        for copy in large(at):
            copy.wait()
        part = jnp.dot(
            x_ref[at].reshape(prompts * rows, depth),
            w_ref[at],
            preferred_element_type=jnp.float32,
        )
        total_ref[...] += part.reshape(total_ref.shape)
        return carry

    early = chunks - chunks // 4
    lax.fori_loop(0, early, accumulate, 0)
    for copy in small:
        copy.wait()
    q_rows = query_ref.shape[1]
    member = lax.axis_index(MEMBERS)
    for distances, packet in zip(PACKETS, packed):
        for to, distance in enumerate(distances):
            for at in range(2):
                head = member ^ distance ^ (SIBLING * at)
                packet[to, at, :q_rows, :] = query_ref[head]
                packet[to, at, q_rows:, :] = recent_ref[head]
    own_prompt = prompt_ref[me]
    earlier = jnp.int32(0)
    for g in range(groups):
        same = jnp.logical_and(g < me, prompt_ref[g] == own_prompt)
        earlier = earlier + jnp.where(same, 1, 0)
    limit = count_ref[own_prompt] - earlier * lax.axis_size(MEMBERS)
    for at, distance in enumerate(PEERS + (0,)):
        live = jnp.where((member ^ distance) < limit, 1.0, 0.0)
        alive_ref[at * q_rows : (at + 1) * q_rows, :] = jnp.full((q_rows, HEAD_DIM), live)
    lax.fori_loop(early, chunks, accumulate, 0)
    for at, out in enumerate(outs):
        prompt = at
        if ordered:
            prompt = prompt_ref[partners(groups)[at][0](me) if at < groups - 1 else me]
        total = total_ref[prompt] + b_ref[...]
        key = total[:, :HEAD_DIM]
        swapped = jnp.concatenate([key[:, half:], key[:, :half]], axis=1)
        out[:, :HEAD_DIM] = (key * cosine + swapped * sine).astype(out.dtype)
        out[:, HEAD_DIM:] = total[:, HEAD_DIM:].astype(out.dtype)


def project(groups, ordered, decode_prompt, sample_counts, prompt_hidden, kv_weight, kv_bias, query, recent):
    prompts, rows, depth = prompt_hidden.shape
    width = kv_weight.shape[1]
    chunks = depth // CHUNK
    packet_shape = (2, query.shape[1] + recent.shape[1], HEAD_DIM)
    packets = [pltpu.VMEM((len(to),) + packet_shape, query.dtype) for to in PACKETS]
    alive = pltpu.VMEM(((len(PEERS) + 1) * query.shape[1], HEAD_DIM), jnp.float32)
    bias = kv_bias.reshape(1, width)
    operands = (decode_prompt, sample_counts, prompt_hidden, kv_weight, bias, query, recent)
    return pl.pallas_call(
        functools.partial(project_kernel, groups, ordered),
        in_specs=[pl.BlockSpec(memory_space=pl.ANY)] * len(operands),
        out_specs=[pl.BlockSpec(memory_space=pltpu.VMEM)] * (prompts + len(packets) + 1),
        out_shape=[pltpu.VMEM((rows, width), jnp.bfloat16)] * prompts + packets + [alive],
        scratch_shapes=[
            pltpu.SMEM(decode_prompt.shape, jnp.int32),
            pltpu.SMEM(sample_counts.shape, jnp.int32),
            pltpu.VMEM((1, width), jnp.float32),
            pltpu.VMEM(query.shape, query.dtype),
            pltpu.VMEM(recent.shape, recent.dtype),
            pltpu.VMEM((chunks, prompts, rows, CHUNK), jnp.bfloat16),
            pltpu.VMEM((chunks, CHUNK, width), jnp.bfloat16),
            pltpu.VMEM((prompts, rows, width), jnp.float32),
            pltpu.SemaphoreType.DMA((5,)),
            pltpu.SemaphoreType.DMA((chunks,)),
            pltpu.SemaphoreType.DMA((chunks,)),
        ],
        compiler_params=pltpu.CompilerParams(vmem_limit_bytes=VMEM_LIMIT),
        name="project",
    )(*map(in_hbm, operands))


def store_kernel(groups, picks, table_ref, *rest):
    blocks, (cache_ref, sem) = rest[: len(picks)], rest[-2:]
    me = lax.axis_index("group")
    pages = blocks[0].shape[0]
    sources = [source(me) for _, source in partners(groups)] + [me]
    for block, at in zip(blocks, picks):

        def place(j, carry, block=block, source=sources[at]):
            slot = table_ref[0, source * pages + j]
            pltpu.make_async_copy(block.at[j], cache_ref.at[slot], sem).start()
            return carry

        lax.fori_loop(0, pages, place, 0, unroll=True)
    stored = cache_ref.at[pl.ds(0, len(picks) * pages)]
    pltpu.make_async_copy(stored, stored, sem).wait()


def store(groups, picks, page_table, blocks, cache=None):
    pages = rows_of(blocks)
    operands = [page_table] + pages
    specs = [pl.BlockSpec(memory_space=pltpu.SMEM)] + [pl.BlockSpec(memory_space=pltpu.VMEM)] * len(pages)
    aliases = {}
    if cache is not None:
        aliases = {len(operands): 0}
        operands.append(cache)
        specs.append(pl.BlockSpec(memory_space=pl.ANY))
    return pl.pallas_call(
        functools.partial(store_kernel, groups, picks),
        in_specs=specs,
        out_specs=pl.BlockSpec(memory_space=pl.ANY),
        out_shape=pltpu.HBM((page_table.shape[1],) + pages[0].shape[1:], jnp.bfloat16),
        input_output_aliases=aliases,
        scratch_shapes=[pltpu.SemaphoreType.DMA],
        cost_estimate=pl.CostEstimate(flops=HIDE_FLOPS, transcendentals=0, bytes_accessed=0),
        compiler_params=pltpu.CompilerParams(vmem_limit_bytes=PACK_VMEM),
        name="store",
    )(*operands)


def rows_of(blocks):
    return [block.reshape(block.shape[0] // PAGE, PAGE, 2 * HEAD_DIM) for block in blocks]


def join_kernel(first_ref, second_ref, out_ref):
    out_ref[0] = first_ref[0]
    out_ref[1] = second_ref[1]


def join(first, second):
    vmem = pl.BlockSpec(memory_space=pltpu.VMEM)
    return pl.pallas_call(
        join_kernel,
        in_specs=[vmem] * 2,
        out_specs=vmem,
        out_shape=pltpu.VMEM(second.shape, second.dtype),
        compiler_params=pltpu.CompilerParams(vmem_limit_bytes=PACK_VMEM),
        name="join",
    )(first, second)


def arrange_kernel(steps, far_ref, near_ref, own_ref, query_ref, key_ref, value_ref):
    packets = (far_ref.at[1], far_ref.at[0], near_ref.at[0], own_ref.at[0])
    q_rows = Q_PER_KV * steps
    for at in range(2):
        recent = jnp.concatenate(
            [packet[at, q_rows:, :].astype(jnp.float32) for packet in packets], axis=0
        )
        shifted = jnp.concatenate([recent[steps:], recent[:steps]], axis=0)
        key_ref[at] = recent.astype(key_ref.dtype)
        value_ref[at] = shifted.astype(value_ref.dtype)
        for sample, packet in enumerate(packets):
            query_ref[at, sample * q_rows : (sample + 1) * q_rows, :] = packet[at, :q_rows, :]


def arrange(steps, packets):
    samples, dtype = len(PEERS) + 1, packets[0].dtype
    vmem = pl.BlockSpec(memory_space=pltpu.VMEM)
    recent = pltpu.VMEM((2, samples * 2 * steps, HEAD_DIM), dtype)
    return pl.pallas_call(
        functools.partial(arrange_kernel, steps),
        in_specs=[vmem] * 3,
        out_specs=[vmem] * 3,
        out_shape=[
            pltpu.VMEM((2, samples * Q_PER_KV * steps, HEAD_DIM), dtype),
            recent,
            recent,
        ],
        cost_estimate=pl.CostEstimate(flops=HIDE_FLOPS, transcendentals=0, bytes_accessed=0),
        compiler_params=pltpu.CompilerParams(vmem_limit_bytes=PACK_VMEM),
        name="arrange",
    )(*packets)


def attend_head(steps, alive, query, recent_key, recent_value, blocks):
    q_rows = Q_PER_KV * steps
    scaling = HEAD_DIM ** (-0.5)
    contract = (((1,), (1,)), ((), ()))

    def scored(keys):
        return (
            lax.dot_general(query, keys, contract, preferred_element_type=jnp.float32) * scaling
        )

    recent_score = scored(recent_key)
    row = lax.broadcasted_iota(jnp.int32, recent_score.shape, 0)
    column = lax.broadcasted_iota(jnp.int32, recent_score.shape, 1)
    visible = jnp.logical_and(
        row // q_rows == column // (2 * steps), column % (2 * steps) <= row % steps
    )
    recent_score = jnp.where(visible, recent_score, -jnp.inf)
    score = scored(jnp.concatenate([block[:, :HEAD_DIM] for block in blocks], axis=0))
    highest = jnp.max(score, axis=1, keepdims=True)
    highest = jnp.maximum(highest, jnp.max(recent_score, axis=1, keepdims=True))
    recent_weight = jnp.exp(recent_score - highest)
    weight = jnp.exp(score - highest)
    total = jnp.sum(weight, axis=1, keepdims=True)
    total = total + jnp.sum(recent_weight, axis=1, keepdims=True)
    values = jnp.concatenate([block[:, HEAD_DIM:] for block in blocks], axis=0)
    blended = jnp.dot(
        recent_weight.astype(jnp.bfloat16), recent_value, preferred_element_type=jnp.float32
    ) + jnp.dot(weight.astype(jnp.bfloat16), values, preferred_element_type=jnp.float32)
    blended = blended / total
    return jnp.where(alive > 0.0, blended, 0.0)


def attend_own_kernel(groups, steps, cache_ref, alive_ref, query_ref, key_ref, value_ref, *rest):
    del cache_ref
    blocks, out_ref = rest[:groups], rest[groups]
    out_ref[...] = attend_head(
        steps,
        alive_ref[...],
        query_ref[0],
        key_ref[0],
        value_ref[0],
        [block[...] for block in blocks],
    ).astype(out_ref.dtype)


def attend_own(groups, steps, cache, alive, arranged, blocks):
    vmem = pl.BlockSpec(memory_space=pltpu.VMEM)
    return pl.pallas_call(
        functools.partial(attend_own_kernel, groups, steps),
        in_specs=[pl.BlockSpec(memory_space=pl.ANY)] + [vmem] * (1 + len(arranged) + groups),
        out_specs=vmem,
        out_shape=pltpu.VMEM(arranged[0].shape[1:], jnp.bfloat16),
        cost_estimate=pl.CostEstimate(flops=HIDE_FLOPS, transcendentals=0, bytes_accessed=0),
        compiler_params=pltpu.CompilerParams(vmem_limit_bytes=VMEM_LIMIT),
        name="attend_own",
    )(in_hbm(cache), alive, *arranged, *blocks)


def attend_kernel(groups, steps, alive_ref, query_ref, key_ref, value_ref, own_ref, *rest):
    blocks, outs = rest[:groups], rest[groups:]
    q_rows = Q_PER_KV * steps
    blended = attend_head(
        steps,
        alive_ref[...],
        query_ref[1],
        key_ref[1],
        value_ref[1],
        [block[...] for block in blocks],
    ).astype(jnp.bfloat16)
    side = jnp.where(lax.axis_index(MEMBERS) & SIBLING == 0, 0, 1)
    for to, out in enumerate(outs):
        out[side] = own_ref[to * q_rows : (to + 1) * q_rows]
        out[1 - side] = blended[to * q_rows : (to + 1) * q_rows]


def attend(groups, steps, alive, arranged, own, blocks):
    packets = len(PEERS) + 1
    vmem = pl.BlockSpec(memory_space=pltpu.VMEM)
    return pl.pallas_call(
        functools.partial(attend_kernel, groups, steps),
        in_specs=[vmem] * (2 + len(arranged) + groups),
        out_specs=[vmem] * packets,
        out_shape=[pltpu.VMEM((2, Q_PER_KV * steps, HEAD_DIM), jnp.bfloat16)] * packets,
        compiler_params=pltpu.CompilerParams(vmem_limit_bytes=VMEM_LIMIT),
        name="attend",
    )(alive, *arranged, own, *blocks)


def gather_kernel(*refs):
    parts, out_ref, sem = refs[:-2], refs[-2], refs[-1]
    member = lax.axis_index(MEMBERS)
    copies = []
    for distance, part in zip(PEERS + (0,), parts):
        head = member ^ distance
        copies.append(
            pltpu.make_async_copy(part, out_ref.at[head // 4, :, head % 2], sem.at[len(copies)])
        )
    for copy in copies:
        copy.start()
    for copy in copies:
        copy.wait()


def gather(parts):
    heads, rows, width = 2 * len(parts), parts[0].shape[1], parts[0].shape[2]
    return pl.pallas_call(
        gather_kernel,
        in_specs=[pl.BlockSpec(memory_space=pltpu.VMEM)] * len(parts),
        out_specs=pl.BlockSpec(memory_space=pl.ANY),
        out_shape=pltpu.HBM((heads // 4, 2, 2, rows, width), parts[0].dtype),
        scratch_shapes=[pltpu.SemaphoreType.DMA((len(parts),))],
        compiler_params=pltpu.CompilerParams(vmem_limit_bytes=PACK_VMEM),
        name="gather",
    )(*parts)


def local(
    prompt_hidden, kv_weight, kv_bias, new_query, new_kv, decode_prompt, sample_counts, page_table
):
    prompts, rows, _ = prompt_hidden.shape
    groups = lax.axis_size("group")
    steps = new_query.shape[2]
    me = lax.axis_index("group")
    ordered = groups == prompts

    by_head = new_query.reshape(steps, KV_HEADS, Q_PER_KV, HEAD_DIM).transpose(1, 2, 0, 3)
    kv_by_head = new_kv.reshape(steps, KV_HEADS, 2, HEAD_DIM).transpose(1, 2, 0, 3)
    results = project(
        groups,
        ordered,
        decode_prompt,
        sample_counts,
        prompt_hidden,
        kv_weight,
        kv_bias,
        by_head.reshape(KV_HEADS, Q_PER_KV * steps, HEAD_DIM),
        kv_by_head.reshape(KV_HEADS, 2 * steps, HEAD_DIM),
    )
    projected, packets, alive = results[:prompts], results[prompts:-1], results[-1]
    if ordered:
        outgoing, own = projected[:-1], projected[-1]
    else:
        pages = jnp.stack(projected)

        def pages_of(group):
            return lax.dynamic_index_in_dim(pages, decode_prompt[group], 0, keepdims=False)

        outgoing = [pages_of(goes_to(me)) for goes_to, _ in partners(groups)]
        own = pages_of(me)
    blocks = [
        lax.ppermute(block, "group", [(i, goes_to(i)) for i in range(groups)])
        for block, (goes_to, _) in zip(outgoing, partners(groups))
    ]
    members = lax.axis_size(MEMBERS)

    def to_peer(array, distance):
        return lax.ppermute(array, MEMBERS, [(i, i ^ distance) for i in range(members)])

    near, far, mine = packets
    near = to_peer(near, NEAR)
    packets = [to_peer(join(far, near), FAR), near, mine]
    blocks = blocks + [own]
    ready = [own] + blocks[:-3] + [blocks[-2], blocks[-3]]
    sibling_blocks = [to_peer(block, SIBLING) for block in ready]
    arranged = arrange(steps, packets)
    early = (groups - 1,)
    cache = store(groups, early, page_table, [blocks[at] for at in early])
    own_head = attend_own(groups, steps, cache, alive, arranged, ready)
    parts = attend(groups, steps, alive, arranged, own_head, sibling_blocks)
    late = tuple(at for at in range(groups) if at not in early)
    cache = store(groups, late, page_table, [blocks[at] for at in late], cache)
    returned = gather([to_peer(part, at) for part, at in zip(parts, PEERS)] + [parts[-1]])
    attention_out = returned.reshape(KV_HEADS * Q_PER_KV, steps, HEAD_DIM).transpose(1, 0, 2)
    return attention_out.reshape(new_query.shape), cache[None]


def solution(mesh):
    return jax.shard_map(
        local,
        mesh=mesh,
        in_specs=(
            P(None, "group", None),
            P(None, MEMBERS),
            P(MEMBERS),
            P("group", MEMBERS, None, None),
            P("group", MEMBERS, None, None),
            P(),
            P(),
            P("group", None),
        ),
        out_specs=(P("group", MEMBERS, None, None), P("group", None, None, MEMBERS)),
        check_vma=False,
    )
```

```python
import functools
import math

import jax
import jax.numpy as jnp
from jax import lax
from jax.experimental import pallas as pl
from jax.experimental.pallas import tpu as pltpu
from jax.sharding import PartitionSpec as P

KV_HEADS = 8
HEAD_DIM = 128
Q_PER_KV = 8
PAGE = 8
ROPE_BASE = 1000000.0
MEMBERS = ("tp", "fork")
CHUNK = 1024
VMEM_LIMIT = 40 * 1024 * 1024
PACK_VMEM = 4 * 1024 * 1024
HIDE_FLOPS = 20 * 10**9


def partners(groups):
    if groups & (groups - 1) == 0:
        return [
            (lambda me, s=s: me ^ s, lambda me, s=s: me ^ s) for s in range(groups - 1, 0, -1)
        ]
    return [
        (lambda me, s=s: (me + s) % groups, lambda me, s=s: (me + groups - s) % groups)
        for s in range(1, groups)
    ]


SIBLING = 2
PEERS = (5, 4, 1)
NEAR, FAR = 1, 4
PACKETS = ((NEAR, NEAR ^ FAR), (FAR,), (0,))


def in_hbm(array):
    return pltpu.with_memory_space_constraint(array, pltpu.HBM)


def project_kernel(
    groups,
    ordered,
    prompt_hbm,
    count_hbm,
    x_hbm,
    w_hbm,
    b_hbm,
    query_hbm,
    recent_hbm,
    *rest,
):
    prompts = x_hbm.shape[0]
    outs, packed, rest = rest[:prompts], rest[prompts : prompts + 3], rest[prompts + 3 :]
    alive_ref, prompt_ref, count_ref, b_ref, query_ref, recent_ref, x_ref, w_ref, total_ref = rest[:9]
    small_sem, x_sem, w_sem = rest[9:]
    chunks, prompts, rows, depth = x_ref.shape
    small = [
        pltpu.make_async_copy(source, target, small_sem.at[at])
        for at, (source, target) in enumerate(
            [
                (prompt_hbm, prompt_ref),
                (count_hbm, count_ref),
                (b_hbm, b_ref),
                (recent_hbm, recent_ref),
                (query_hbm, query_ref),
            ]
        )
    ]

    def large(at):
        begin = pl.multiple_of(at * depth, depth)
        return (
            pltpu.make_async_copy(w_hbm.at[pl.ds(begin, depth)], w_ref.at[at], w_sem.at[at]),
            pltpu.make_async_copy(x_hbm.at[:, :, pl.ds(begin, depth)], x_ref.at[at], x_sem.at[at]),
        )

    for copy in small:
        copy.start()
    for at in range(chunks):
        for copy in large(at):
            copy.start()

    me = lax.axis_index("group")
    half = HEAD_DIM // 2
    lane = lax.broadcasted_iota(jnp.int32, (rows, HEAD_DIM), 1)
    index = jnp.where(lane < half, lane, lane - half).astype(jnp.float32)
    frequency = jnp.exp(index * (-2.0 * math.log(ROPE_BASE) / HEAD_DIM))
    position = me * rows + lax.broadcasted_iota(jnp.int32, (rows, HEAD_DIM), 0)
    angle = position.astype(jnp.float32) * frequency
    cosine = jnp.cos(angle)
    sine = jnp.sin(angle)
    sine = jnp.where(lane < half, -sine, sine)
    total_ref[...] = jnp.zeros_like(total_ref)

    def accumulate(at, carry):
        for copy in large(at):
            copy.wait()
        part = jnp.dot(
            x_ref[at].reshape(prompts * rows, depth),
            w_ref[at],
            preferred_element_type=jnp.float32,
        )
        total_ref[...] += part.reshape(total_ref.shape)
        return carry

    early = chunks - chunks // 4
    lax.fori_loop(0, early, accumulate, 0)
    for copy in small:
        copy.wait()
    q_rows = query_ref.shape[1]
    member = lax.axis_index(MEMBERS)
    for distances, packet in zip(PACKETS, packed):
        for to, distance in enumerate(distances):
            for at in range(2):
                head = member ^ distance ^ (SIBLING * at)
                packet[to, at, :q_rows, :] = query_ref[head]
                packet[to, at, q_rows:, :] = recent_ref[head]
    own_prompt = prompt_ref[me]
    earlier = jnp.int32(0)
    for g in range(groups):
        same = jnp.logical_and(g < me, prompt_ref[g] == own_prompt)
        earlier = earlier + jnp.where(same, 1, 0)
    limit = count_ref[own_prompt] - earlier * lax.axis_size(MEMBERS)
    for at, distance in enumerate(PEERS + (0,)):
        live = jnp.where((member ^ distance) < limit, 1.0, 0.0)
        alive_ref[at * q_rows : (at + 1) * q_rows, :] = jnp.full((q_rows, HEAD_DIM), live)
    lax.fori_loop(early, chunks, accumulate, 0)
    for at, out in enumerate(outs):
        prompt = at
        if ordered:
            prompt = prompt_ref[partners(groups)[at][0](me) if at < groups - 1 else me]
        total = total_ref[prompt] + b_ref[...]
        key = total[:, :HEAD_DIM]
        swapped = jnp.concatenate([key[:, half:], key[:, :half]], axis=1)
        out[:, :HEAD_DIM] = (key * cosine + swapped * sine).astype(out.dtype)
        out[:, HEAD_DIM:] = total[:, HEAD_DIM:].astype(out.dtype)


def project(groups, ordered, decode_prompt, sample_counts, prompt_hidden, kv_weight, kv_bias, query, recent):
    prompts, rows, depth = prompt_hidden.shape
    width = kv_weight.shape[1]
    chunks = depth // CHUNK
    packet_shape = (2, query.shape[1] + recent.shape[1], HEAD_DIM)
    packets = [pltpu.VMEM((len(to),) + packet_shape, query.dtype) for to in PACKETS]
    alive = pltpu.VMEM(((len(PEERS) + 1) * query.shape[1], HEAD_DIM), jnp.float32)
    bias = kv_bias.reshape(1, width)
    operands = (decode_prompt, sample_counts, prompt_hidden, kv_weight, bias, query, recent)
    return pl.pallas_call(
        functools.partial(project_kernel, groups, ordered),
        in_specs=[pl.BlockSpec(memory_space=pl.ANY)] * len(operands),
        out_specs=[pl.BlockSpec(memory_space=pltpu.VMEM)] * (prompts + len(packets) + 1),
        out_shape=[pltpu.VMEM((rows, width), jnp.bfloat16)] * prompts + packets + [alive],
        scratch_shapes=[
            pltpu.SMEM(decode_prompt.shape, jnp.int32),
            pltpu.SMEM(sample_counts.shape, jnp.int32),
            pltpu.VMEM((1, width), jnp.float32),
            pltpu.VMEM(query.shape, query.dtype),
            pltpu.VMEM(recent.shape, recent.dtype),
            pltpu.VMEM((chunks, prompts, rows, CHUNK), jnp.bfloat16),
            pltpu.VMEM((chunks, CHUNK, width), jnp.bfloat16),
            pltpu.VMEM((prompts, rows, width), jnp.float32),
            pltpu.SemaphoreType.DMA((5,)),
            pltpu.SemaphoreType.DMA((chunks,)),
            pltpu.SemaphoreType.DMA((chunks,)),
        ],
        compiler_params=pltpu.CompilerParams(vmem_limit_bytes=VMEM_LIMIT),
        name="project",
    )(*map(in_hbm, operands))


def store_kernel(groups, picks, table_ref, *rest):
    blocks, (cache_ref, sem) = rest[: len(picks)], rest[-2:]
    me = lax.axis_index("group")
    pages = blocks[0].shape[0]
    sources = [source(me) for _, source in partners(groups)] + [me]
    for block, at in zip(blocks, picks):

        def place(j, carry, block=block, source=sources[at]):
            slot = table_ref[0, source * pages + j]
            pltpu.make_async_copy(block.at[j], cache_ref.at[slot], sem).start()
            return carry

        lax.fori_loop(0, pages, place, 0, unroll=True)
    stored = cache_ref.at[pl.ds(0, len(picks) * pages)]
    pltpu.make_async_copy(stored, stored, sem).wait()


def store(groups, picks, page_table, blocks, cache=None):
    pages = rows_of(blocks)
    operands = [page_table] + pages
    specs = [pl.BlockSpec(memory_space=pltpu.SMEM)] + [pl.BlockSpec(memory_space=pltpu.VMEM)] * len(pages)
    aliases = {}
    if cache is not None:
        aliases = {len(operands): 0}
        operands.append(cache)
        specs.append(pl.BlockSpec(memory_space=pl.ANY))
    return pl.pallas_call(
        functools.partial(store_kernel, groups, picks),
        in_specs=specs,
        out_specs=pl.BlockSpec(memory_space=pl.ANY),
        out_shape=pltpu.HBM((page_table.shape[1],) + pages[0].shape[1:], jnp.bfloat16),
        input_output_aliases=aliases,
        scratch_shapes=[pltpu.SemaphoreType.DMA],
        cost_estimate=pl.CostEstimate(flops=HIDE_FLOPS, transcendentals=0, bytes_accessed=0),
        compiler_params=pltpu.CompilerParams(vmem_limit_bytes=PACK_VMEM),
        name="store",
    )(*operands)


def rows_of(blocks):
    return [block.reshape(block.shape[0] // PAGE, PAGE, 2 * HEAD_DIM) for block in blocks]


def join_kernel(first_ref, second_ref, out_ref):
    out_ref[0] = first_ref[0]
    out_ref[1] = second_ref[1]


def join(first, second):
    vmem = pl.BlockSpec(memory_space=pltpu.VMEM)
    return pl.pallas_call(
        join_kernel,
        in_specs=[vmem] * 2,
        out_specs=vmem,
        out_shape=pltpu.VMEM(second.shape, second.dtype),
        compiler_params=pltpu.CompilerParams(vmem_limit_bytes=PACK_VMEM),
        name="join",
    )(first, second)


def arrange_kernel(steps, far_ref, near_ref, own_ref, query_ref, key_ref, value_ref, mask_ref):
    packets = (far_ref.at[1], far_ref.at[0], near_ref.at[0], own_ref.at[0])
    q_rows = Q_PER_KV * steps
    row = lax.broadcasted_iota(jnp.int32, mask_ref.shape, 0)
    column = lax.broadcasted_iota(jnp.int32, mask_ref.shape, 1)
    visible = jnp.logical_and(
        row // q_rows == column // (2 * steps), column % (2 * steps) <= row % steps
    )
    mask_ref[...] = jnp.where(visible, 0.0, -jnp.inf)
    for at in range(2):
        recent = jnp.concatenate(
            [packet[at, q_rows:, :].astype(jnp.float32) for packet in packets], axis=0
        )
        shifted = jnp.concatenate([recent[steps:], recent[:steps]], axis=0)
        key_ref[at] = recent.astype(key_ref.dtype)
        value_ref[at] = shifted.astype(value_ref.dtype)
        for sample, packet in enumerate(packets):
            query_ref[at, sample * q_rows : (sample + 1) * q_rows, :] = packet[at, :q_rows, :]


def arrange(steps, packets):
    samples, dtype = len(PEERS) + 1, packets[0].dtype
    vmem = pl.BlockSpec(memory_space=pltpu.VMEM)
    recent = pltpu.VMEM((2, samples * 2 * steps, HEAD_DIM), dtype)
    return pl.pallas_call(
        functools.partial(arrange_kernel, steps),
        in_specs=[vmem] * 3,
        out_specs=[vmem] * 4,
        out_shape=[
            pltpu.VMEM((2, samples * Q_PER_KV * steps, HEAD_DIM), dtype),
            recent,
            recent,
            pltpu.VMEM((samples * Q_PER_KV * steps, samples * 2 * steps), jnp.float32),
        ],
        cost_estimate=pl.CostEstimate(flops=HIDE_FLOPS, transcendentals=0, bytes_accessed=0),
        compiler_params=pltpu.CompilerParams(vmem_limit_bytes=PACK_VMEM),
        name="arrange",
    )(*packets)


def attend_head(alive, query, recent_key, recent_value, mask, blocks):
    scaling = HEAD_DIM ** (-0.5)
    contract = (((1,), (1,)), ((), ()))

    def scored(keys):
        return (
            lax.dot_general(query, keys, contract, preferred_element_type=jnp.float32) * scaling
        )

    recent_score = scored(recent_key)
    recent_score = recent_score + mask
    score = scored(jnp.concatenate([block[:, :HEAD_DIM] for block in blocks], axis=0))
    highest = jnp.max(score, axis=1, keepdims=True)
    highest = jnp.maximum(highest, jnp.max(recent_score, axis=1, keepdims=True))
    recent_weight = jnp.exp(recent_score - highest)
    weight = jnp.exp(score - highest)
    total = jnp.sum(weight, axis=1, keepdims=True)
    total = total + jnp.sum(recent_weight, axis=1, keepdims=True)
    values = jnp.concatenate([block[:, HEAD_DIM:] for block in blocks], axis=0)
    blended = jnp.dot(
        recent_weight.astype(jnp.bfloat16), recent_value, preferred_element_type=jnp.float32
    ) + jnp.dot(weight.astype(jnp.bfloat16), values, preferred_element_type=jnp.float32)
    blended = blended / total
    return jnp.where(alive > 0.0, blended, 0.0)


def attend_own_kernel(groups, steps, cache_ref, alive_ref, query_ref, key_ref, value_ref, mask_ref, *rest):
    del cache_ref
    blocks, out_ref = rest[:groups], rest[groups]
    out_ref[...] = attend_head(
        alive_ref[...],
        query_ref[0],
        key_ref[0],
        value_ref[0],
        mask_ref[...],
        [block[...] for block in blocks],
    ).astype(out_ref.dtype)


def attend_own(groups, steps, cache, alive, arranged, blocks):
    vmem = pl.BlockSpec(memory_space=pltpu.VMEM)
    return pl.pallas_call(
        functools.partial(attend_own_kernel, groups, steps),
        in_specs=[pl.BlockSpec(memory_space=pl.ANY)] + [vmem] * (1 + len(arranged) + groups),
        out_specs=vmem,
        out_shape=pltpu.VMEM(arranged[0].shape[1:], jnp.bfloat16),
        cost_estimate=pl.CostEstimate(flops=HIDE_FLOPS, transcendentals=0, bytes_accessed=0),
        compiler_params=pltpu.CompilerParams(vmem_limit_bytes=VMEM_LIMIT),
        name="attend_own",
    )(in_hbm(cache), alive, *arranged, *blocks)


def attend_kernel(groups, steps, alive_ref, query_ref, key_ref, value_ref, mask_ref, own_ref, *rest):
    blocks, outs = rest[:groups], rest[groups:]
    q_rows = Q_PER_KV * steps
    blended = attend_head(
        alive_ref[...],
        query_ref[1],
        key_ref[1],
        value_ref[1],
        mask_ref[...],
        [block[...] for block in blocks],
    ).astype(jnp.bfloat16)
    side = jnp.where(lax.axis_index(MEMBERS) & SIBLING == 0, 0, 1)
    for to, out in enumerate(outs):
        out[side] = own_ref[to * q_rows : (to + 1) * q_rows]
        out[1 - side] = blended[to * q_rows : (to + 1) * q_rows]


def attend(groups, steps, alive, arranged, own, blocks):
    packets = len(PEERS) + 1
    vmem = pl.BlockSpec(memory_space=pltpu.VMEM)
    return pl.pallas_call(
        functools.partial(attend_kernel, groups, steps),
        in_specs=[vmem] * (2 + len(arranged) + groups),
        out_specs=[vmem] * packets,
        out_shape=[pltpu.VMEM((2, Q_PER_KV * steps, HEAD_DIM), jnp.bfloat16)] * packets,
        compiler_params=pltpu.CompilerParams(vmem_limit_bytes=VMEM_LIMIT),
        name="attend",
    )(alive, *arranged, own, *blocks)


def gather_kernel(*refs):
    parts, out_ref, sem = refs[:-2], refs[-2], refs[-1]
    member = lax.axis_index(MEMBERS)
    copies = []
    for distance, part in zip(PEERS + (0,), parts):
        head = member ^ distance
        copies.append(
            pltpu.make_async_copy(part, out_ref.at[head // 4, :, head % 2], sem.at[len(copies)])
        )
    for copy in copies:
        copy.start()
    for copy in copies:
        copy.wait()


def gather(parts):
    heads, rows, width = 2 * len(parts), parts[0].shape[1], parts[0].shape[2]
    return pl.pallas_call(
        gather_kernel,
        in_specs=[pl.BlockSpec(memory_space=pltpu.VMEM)] * len(parts),
        out_specs=pl.BlockSpec(memory_space=pl.ANY),
        out_shape=pltpu.HBM((heads // 4, 2, 2, rows, width), parts[0].dtype),
        scratch_shapes=[pltpu.SemaphoreType.DMA((len(parts),))],
        compiler_params=pltpu.CompilerParams(vmem_limit_bytes=PACK_VMEM),
        name="gather",
    )(*parts)


def local(
    prompt_hidden, kv_weight, kv_bias, new_query, new_kv, decode_prompt, sample_counts, page_table
):
    prompts, rows, _ = prompt_hidden.shape
    groups = lax.axis_size("group")
    steps = new_query.shape[2]
    me = lax.axis_index("group")
    ordered = groups == prompts

    by_head = new_query.reshape(steps, KV_HEADS, Q_PER_KV, HEAD_DIM).transpose(1, 2, 0, 3)
    kv_by_head = new_kv.reshape(steps, KV_HEADS, 2, HEAD_DIM).transpose(1, 2, 0, 3)
    results = project(
        groups,
        ordered,
        decode_prompt,
        sample_counts,
        prompt_hidden,
        kv_weight,
        kv_bias,
        by_head.reshape(KV_HEADS, Q_PER_KV * steps, HEAD_DIM),
        kv_by_head.reshape(KV_HEADS, 2 * steps, HEAD_DIM),
    )
    projected, packets, alive = results[:prompts], results[prompts:-1], results[-1]
    if ordered:
        outgoing, own = projected[:-1], projected[-1]
    else:
        pages = jnp.stack(projected)

        def pages_of(group):
            return lax.dynamic_index_in_dim(pages, decode_prompt[group], 0, keepdims=False)

        outgoing = [pages_of(goes_to(me)) for goes_to, _ in partners(groups)]
        own = pages_of(me)
    blocks = [
        lax.ppermute(block, "group", [(i, goes_to(i)) for i in range(groups)])
        for block, (goes_to, _) in zip(outgoing, partners(groups))
    ]
    members = lax.axis_size(MEMBERS)

    def to_peer(array, distance):
        return lax.ppermute(array, MEMBERS, [(i, i ^ distance) for i in range(members)])

    near, far, mine = packets
    near = to_peer(near, NEAR)
    packets = [to_peer(join(far, near), FAR), near, mine]
    blocks = blocks + [own]
    ready = [own] + blocks[:-3] + [blocks[-2], blocks[-3]]
    sibling_blocks = [to_peer(block, SIBLING) for block in ready]
    arranged = arrange(steps, packets)
    early = (groups - 1,)
    cache = store(groups, early, page_table, [blocks[at] for at in early])
    own_head = attend_own(groups, steps, cache, alive, arranged, ready)
    parts = attend(groups, steps, alive, arranged, own_head, sibling_blocks)
    late = tuple(at for at in range(groups) if at not in early)
    cache = store(groups, late, page_table, [blocks[at] for at in late], cache)
    returned = gather([to_peer(part, at) for part, at in zip(parts, PEERS)] + [parts[-1]])
    attention_out = returned.reshape(KV_HEADS * Q_PER_KV, steps, HEAD_DIM).transpose(1, 0, 2)
    return attention_out.reshape(new_query.shape), cache[None]


def solution(mesh):
    return jax.shard_map(
        local,
        mesh=mesh,
        in_specs=(
            P(None, "group", None),
            P(None, MEMBERS),
            P(MEMBERS),
            P("group", MEMBERS, None, None),
            P("group", MEMBERS, None, None),
            P(),
            P(),
            P("group", None),
        ),
        out_specs=(P("group", MEMBERS, None, None), P("group", None, None, MEMBERS)),
        check_vma=False,
    )
```
